1024 devices in a mesh: gx: 16 (over x, y_lo), gy: 64 (over z, y_hi, core).
Axes of the slice: x: 8, y: 8 (y_hi: 4, y_lo: 2; y = y_hi * 2 + y_lo), z: 8, core: 2. Of those that a mesh axis runs over, the one named last changes fastest.
Arguments:
- velocity: float32 [3, 128, 512, 128], P(None, 'gx', 'gy'), may hold values from -6 to 6
- stress: float32 [6, 128, 512, 128], P(None, 'gx', 'gy'), may hold values from -6 to 6
- memory: float32 [6, 128, 512, 128], P(None, 'gx', 'gy'), may hold values from -4 to 4
- material: float32 [3, 128, 512, 128], P(None, 'gx', 'gy'), may hold values from 0.5 to 1.5
- anelastic: float32 [2, 128, 512, 128], P(None, 'gx', 'gy'), may hold values from 0.3 to 0.9
- zone_ids: int32 [128, 512, 128], P('gx', 'gy'), may hold values from 0 to 7
- absorb_mask: int32 [128, 512, 128], P('gx', 'gy'), may hold values 0 or 1
- source_cells: int32 [16, 64, 128], P('gx', 'gy'), may hold values from 0 to 8191
- source_moment: float32 [16, 64, 6, 128], P('gx', 'gy'), may hold values from -6 to 6
- cohesion_table: float32 [8], replicated, may hold values from 0.6 to 1.6
- friction_table: float32 [8], replicated, may hold values from 0.1 to 0.7
Outputs:
- velocity_out: float32 [3, 128, 512, 128], P(None, 'gx', 'gy')
- stress_out: float32 [6, 128, 512, 128], P(None, 'gx', 'gy')
- memory_out: float32 [6, 128, 512, 128], P(None, 'gx', 'gy')
The draws below stay inside these ranges and needn't reach their ends.
Inputs may be any that keep to these rules, and one draw needn't show every extreme that they name: `source_cells`: p encodes the local cell (p // 1024, (p // 128) % 8, p % 128) of the device's block; several sources may share a cell.
All inputs are finite; a program needn't handle non-finite values. No bound on the sum of `absorb_mask` on one device may be relied on, other than what follows from the above.
Results may differ from the reference program's by a relative error of at most 0.00002.
Values sent between devices are 32-bit elements; how exact they have to be, the bound alone decides.
A program may use at most 32 MiB of HBM per device.

```python
import jax
import jax.numpy as jnp

CX = 8
CY = 8
CZ = 128
STEPS = 2
ZONES = 8
SRC = 128
NX = 128
NY = 512
NZ = 128
N_GX = 16
N_GY = 64


def plant(entries, stream_key, low, largest):
    index_at = [jax.random.randint(jax.random.fold_in(stream_key, axis), (), 0, length) for axis, length in enumerate(entries.shape)]
    main_axis = entries.shape.index(max(entries.shape))
    next_to = index_at[:main_axis] + [(index_at[main_axis] + 1) % entries.shape[main_axis]] + index_at[main_axis + 1:]
    return entries.at[tuple(index_at)].set(low).at[tuple(next_to)].set(largest)


def block_scale(rng, extent, split, low, largest):
    gain = 1.0
    for axis_at, parts in split:
        steps = jax.random.uniform(jax.random.fold_in(jax.random.fold_in(rng, 6), axis_at), (parts,), jnp.float32, low / len(split), largest / len(split))
        gain = gain * jnp.repeat(jnp.exp(steps), extent[axis_at] // parts).reshape((-1,) + (1,) * (len(extent) - 1 - axis_at))
    return gain


def gaussian(rng, dims, deviation, most, shards=(), kind=jnp.bfloat16):
    entries = deviation * jax.random.normal(rng, dims, jnp.float32)
    if shards:
        entries = entries * block_scale(rng, dims, shards, -0.22, 0.18)
    return jnp.clip(entries, -most, most).astype(kind)


def setup_inputs(seed: int = 0) -> dict:
    splits = jax.random.split(jax.random.key(seed), 12)
    velocity = gaussian(splits[0], (3, NX, NY, NZ), 1.0, 6.0, ((1, 16), (2, 64)), jnp.float32)
    stress = gaussian(splits[1], (6, NX, NY, NZ), 1.0, 6.0, ((1, 16), (2, 64)), jnp.float32)
    memory = gaussian(splits[2], (6, NX, NY, NZ), 0.5, 4.0, ((1, 16), (2, 64)), jnp.float32)
    material = jnp.clip(0.5 + 1.0 * jax.random.uniform(splits[3], (3, NX, NY, NZ), jnp.float32) ** block_scale(splits[3], (3, NX, NY, NZ), ((1, 16), (2, 64)), -0.2, 0.2), 0.5, 1.5)
    anelastic = jnp.clip(0.3 + 0.59999996 * jax.random.uniform(splits[4], (2, NX, NY, NZ), jnp.float32) ** block_scale(splits[4], (2, NX, NY, NZ), ((1, 16), (2, 64)), -0.2, 0.2), 0.3, 0.9)
    zone_ids = plant(jax.random.randint(splits[5], (NX, NY, NZ), 0, ZONES), jax.random.fold_in(splits[5], 1), 0, ZONES - 1).astype(jnp.int32)
    absorb_mask = plant((jax.random.randint(splits[6], (NX, NY, NZ), 0, 4) < 1).astype(jnp.int32), jax.random.fold_in(splits[6], 1), 0, 1)
    source_cells = plant(jax.random.randint(splits[7], (N_GX, N_GY, SRC), 0, CX * CY * CZ), jax.random.fold_in(splits[7], 1), 0, (CX * CY * CZ) - 1).astype(jnp.int32)
    source_moment = gaussian(splits[8], (N_GX, N_GY, 6, SRC), 1.0, 6.0, ((0, 16), (1, 64)), jnp.float32)
    cohesion_table = jnp.clip(jax.random.uniform(splits[9], (ZONES,), jnp.float32, 0.6, 1.6), 0.6, 1.6)
    friction_table = jnp.clip(jax.random.uniform(splits[10], (ZONES,), jnp.float32, 0.1, 0.7), 0.1, 0.7)
    return {"velocity": velocity, "stress": stress, "memory": memory, "material": material, "anelastic": anelastic, "zone_ids": zone_ids, "absorb_mask": absorb_mask, "source_cells": source_cells, "source_moment": source_moment, "cohesion_table": cohesion_table, "friction_table": friction_table}


coef_near = 9.0 / 8.0
coef_far = -1.0 / 24.0
time_ratio = 0.12
sponge_factor = 0.92

def shifted(field, margin, keep_cycle, shift_x, shift_y, shift_z):
    out_x = field.shape[-3] - 2 * margin + 2 * keep_cycle
    out_y = field.shape[-2] - 2 * margin + 2 * keep_cycle
    out_z = field.shape[-1] - 4
    start_x = margin + shift_x - keep_cycle
    start_y = margin + shift_y - keep_cycle
    start_z = 2 + shift_z
    return field[..., start_x:start_x + out_x, start_y:start_y + out_y, start_z:start_z + out_z]

def offset_view(field, margin, keep_cycle, axis, amount):
    shifts = [0, 0, 0]
    shifts[axis] = amount
    return shifted(field, margin, keep_cycle, shifts[0], shifts[1], shifts[2])

def forward(field, margin, keep_cycle, axis):
    return coef_near * (offset_view(field, margin, keep_cycle, axis, 1) - offset_view(field, margin, keep_cycle, axis, 0)) + coef_far * (offset_view(field, margin, keep_cycle, axis, 2) - offset_view(field, margin, keep_cycle, axis, -1))

def backward(field, margin, keep_cycle, axis):
    return coef_near * (offset_view(field, margin, keep_cycle, axis, 0) - offset_view(field, margin, keep_cycle, axis, -1)) + coef_far * (offset_view(field, margin, keep_cycle, axis, 1) - offset_view(field, margin, keep_cycle, axis, -2))

def pad_depth(field):
    return jnp.pad(field, [(0, 0)] * (field.ndim - 1) + [(2, 2)])

def velocity_step(stress_pad, margin, keep_cycle, velocity, buoyancy, damping):
    rate_x = forward(stress_pad[0], margin, keep_cycle, 0) + backward(stress_pad[3], margin, keep_cycle, 1) + backward(stress_pad[4], margin, keep_cycle, 2)
    rate_y = backward(stress_pad[3], margin, keep_cycle, 0) + forward(stress_pad[1], margin, keep_cycle, 1) + backward(stress_pad[5], margin, keep_cycle, 2)
    rate_z = backward(stress_pad[4], margin, keep_cycle, 0) + backward(stress_pad[5], margin, keep_cycle, 1) + forward(stress_pad[2], margin, keep_cycle, 2)
    rates = jnp.stack([rate_x, rate_y, rate_z], axis=0)
    return (velocity + time_ratio * buoyancy * rates) * damping

def stress_step(velocity_pad, stress, memory, material, anelastic):
    strain_xx = backward(velocity_pad[0], 2, 0, 0)
    strain_yy = backward(velocity_pad[1], 2, 0, 1)
    strain_zz = backward(velocity_pad[2], 2, 0, 2)
    strain_xy = forward(velocity_pad[0], 2, 0, 1) + forward(velocity_pad[1], 2, 0, 0)
    strain_xz = forward(velocity_pad[0], 2, 0, 2) + forward(velocity_pad[2], 2, 0, 0)
    strain_yz = forward(velocity_pad[1], 2, 0, 2) + forward(velocity_pad[2], 2, 0, 1)
    lame = material[0]
    modulus = material[1]
    volume = strain_xx + strain_yy + strain_zz
    increment = time_ratio * jnp.stack([lame * volume + 2.0 * modulus * strain_xx, lame * volume + 2.0 * modulus * strain_yy, lame * volume + 2.0 * modulus * strain_zz, modulus * strain_xy, modulus * strain_xz, modulus * strain_yz], axis=0)
    memory_new = anelastic[0] * memory + anelastic[1] * increment
    trial = stress + increment - 0.5 * (memory + memory_new)
    return (trial, memory_new)

def zone_values(zone_ids, cohesion_table, friction_table):
    cohesion = jnp.zeros(zone_ids.shape, jnp.float32)
    friction = jnp.zeros(zone_ids.shape, jnp.float32)
    for zone in range(ZONES):
        inside = zone_ids == zone
        cohesion = cohesion + jnp.where(inside, cohesion_table[zone], 0.0)
        friction = friction + jnp.where(inside, friction_table[zone], 0.0)
    return (cohesion, friction)

def add_sources(trial, flat_index, amplitude):
    shape = trial.shape
    flat = trial.reshape(6, -1)
    flat = flat.at[:, flat_index].add(time_ratio * amplitude)
    return flat.reshape(shape)

def yield_limit(trial, cohesion, friction):
    mean_stress = (trial[0] + trial[1] + trial[2]) / 3.0
    return jnp.maximum(cohesion - friction * mean_stress, 0.25 * cohesion)

def below(field):
    return jnp.pad(field, ((0, 0), (0, 0), (1, 0)))[..., :-1]

def above(field):
    return jnp.pad(field, ((0, 0), (0, 0), (0, 1)))[..., 1:]

def plastic_step(extended, trial, upper_x, upper_y):
    size_x = trial.shape[1]
    size_y = trial.shape[2]
    centre = extended[:, 1:, 1:, :]
    mean_stress = (centre[0] + centre[1] + centre[2]) / 3.0
    dev_xx = centre[0] - mean_stress
    dev_yy = centre[1] - mean_stress
    dev_zz = centre[2] - mean_stress
    shear_xy = extended[3]
    centre_xy = 0.25 * (shear_xy[:-1, :-1] + shear_xy[:-1, 1:] + shear_xy[1:, :-1] + shear_xy[1:, 1:])
    lower_xz = extended[4][:-1, 1:]
    upper_xz = extended[4][1:, 1:]
    centre_xz = 0.25 * (lower_xz + below(lower_xz) + upper_xz + below(upper_xz))
    lower_yz = extended[5][1:, :-1]
    upper_yz = extended[5][1:, 1:]
    centre_yz = 0.25 * (lower_yz + below(lower_yz) + upper_yz + below(upper_yz))
    tau = jnp.sqrt(0.5 * (dev_xx * dev_xx + dev_yy * dev_yy + dev_zz * dev_zz) + centre_xy * centre_xy + centre_xz * centre_xz + centre_yz * centre_yz)
    ratio = jnp.minimum(1.0, centre[6] / jnp.maximum(tau, 0.5))
    valid_x = jnp.where(jnp.arange(size_x + 1) < size_x, 1.0, upper_x).astype(jnp.float32)
    valid_y = jnp.where(jnp.arange(size_y + 1) < size_y, 1.0, upper_y).astype(jnp.float32)
    deficit = (1.0 - ratio) * valid_x[:, None, None] * valid_y[None, :, None]
    factor_xy = 1.0 - 0.25 * (deficit[:-1, :-1] + deficit[1:, :-1] + deficit[:-1, 1:] + deficit[1:, 1:])
    first_xz = deficit[:-1, :-1]
    second_xz = deficit[1:, :-1]
    factor_xz = 1.0 - 0.25 * (first_xz + above(first_xz) + second_xz + above(second_xz))
    first_yz = deficit[:-1, :-1]
    second_yz = deficit[:-1, 1:]
    factor_yz = 1.0 - 0.25 * (first_yz + above(first_yz) + second_yz + above(second_yz))
    inner_mean = mean_stress[:-1, :-1]
    inner_ratio = ratio[:-1, :-1]
    return jnp.stack([inner_mean + inner_ratio * dev_xx[:-1, :-1], inner_mean + inner_ratio * dev_yy[:-1, :-1], inner_mean + inner_ratio * dev_zz[:-1, :-1], factor_xy * trial[3], factor_xz * trial[4], factor_yz * trial[5]], axis=0)

def reference(velocity, stress, memory, material, anelastic, zone_ids, absorb_mask, source_cells, source_moment, cohesion_table, friction_table):
    damping = jnp.where(absorb_mask == 1, sponge_factor, 1.0).astype(jnp.float32)
    buoyancy = material[2]
    cohesion, friction = zone_values(zone_ids, cohesion_table, friction_table)
    device_x = jnp.arange(N_GX, dtype=jnp.int32)[:, None, None]
    device_y = jnp.arange(N_GY, dtype=jnp.int32)[None, :, None]
    place_x = device_x * CX + source_cells // (CY * CZ)
    place_y = device_y * CY + source_cells // CZ % CY
    place_z = source_cells % CZ
    flat_index = ((place_x * NY + place_y) * NZ + place_z).reshape(-1).astype(jnp.int32)
    amplitude = jnp.moveaxis(source_moment, 2, 0).reshape(6, -1)
    for time_step in range(STEPS):
        stress_pad = pad_depth(jnp.pad(stress, ((0, 0), (2, 2), (2, 2), (0, 0))))
        velocity = velocity_step(stress_pad, 2, 0, velocity, buoyancy, damping)
        velocity_pad = pad_depth(jnp.pad(velocity, ((0, 0), (2, 2), (2, 2), (0, 0))))
        trial, memory = stress_step(velocity_pad, stress, memory, material, anelastic)
        trial = add_sources(trial, flat_index, amplitude)
        limit = yield_limit(trial, cohesion, friction)
        extended = jnp.pad(jnp.concatenate([trial, limit[None]], axis=0), ((0, 0), (1, 1), (1, 1), (0, 0)))
        stress = plastic_step(extended, trial, 0.0, 0.0)
    return (velocity, stress, memory)
```

```python
import functools

import jax
import jax.numpy as jnp
from jax import lax
from jax.experimental import pallas as pl
from jax.experimental.pallas import tpu as pltpu
from jax.sharding import PartitionSpec as P

MESH = pl.DeviceIdType.MESH
STEPS = 2
ZONES = 8
NEAR = 9.0 / 8.0
FAR = -1.0 / 24.0
H = 0.12
SPONGE = 0.92
OPEN = 1.0e9

SXX, SXY, SXZ, SYY, SYZ, VX, VY, VZ = range(8)
CXX, CYY, CZZ, CXY, CXZ, CYZ = range(8, 14)
PP, QQ, COH, FRI = range(14, 18)
TXY, UXZ, UYZ, DEF, DEZ = range(18, 23)
FIELDS = 23
SLABS = 14
PITCH = 16

FACES = ((-1, 0), (1, 0), (0, -1), (0, 1))
CORNERS = ((-1, -1), (-1, 1), (1, -1), (1, 1))
SIDES = FACES + CORNERS


def row(x, y):
    return (x + 3) * PITCH + (y + 4)


def xs(field, x):
    return (field, "B", x, 0, 8)


def ys(field, y):
    return (field, "F", 0, y, 8)


def some(field, x, y, n=1):
    return (field, "B", x, y, n)


STRESS_SENT = {
    (1, 0): [xs(SXX, 7), xs(SXY, 6), xs(SXY, 7), xs(SXZ, 6), xs(SXZ, 7)],
    (-1, 0): [xs(SXX, 0), xs(SXX, 1), xs(SXY, 0), xs(SXZ, 0)],
    (0, 1): [ys(SYY, 7), ys(SXY, 6), ys(SXY, 7), ys(SYZ, 6), ys(SYZ, 7)],
    (0, -1): [ys(SYY, 0), ys(SYY, 1), ys(SXY, 0), ys(SYZ, 0)],
}
BASE_SENT = {
    (1, 0): [xs(CXY, 7), xs(CXZ, 7)],
    (-1, 0): [xs(f, 0) for f in (CXX, CYY, CZZ, CXY, CXZ, CYZ)],
    (0, 1): [ys(CXY, 7), ys(CYZ, 7)],
    (0, -1): [ys(f, 0) for f in (CXX, CYY, CZZ, CXY, CXZ, CYZ)],
}
FIXED_SENT = {
    (1, 0): [xs(QQ, 7)],
    (-1, 0): [xs(f, 0) for f in (PP, QQ, COH, FRI)],
    (0, 1): [ys(QQ, 7)],
    (0, -1): [ys(f, 0) for f in (PP, QQ, COH, FRI)],
    (1, 1): [some(QQ, 7, 7)],
    (-1, -1): [some(f, 0, 0) for f in (PP, QQ, COH, FRI)],
    (-1, 1): [some(QQ, 0, 7)],
    (1, -1): [some(QQ, 7, 0)],
}
VELOCITY_SENT = {
    (1, 0): [xs(f, x) for f in (VX, VY, VZ) for x in (6, 7)],
    (-1, 0): [xs(f, x) for f, n in ((VX, 2), (VY, 3), (VZ, 3)) for x in range(n)],
    (0, 1): [ys(f, y) for f in (VX, VY, VZ) for y in (6, 7)],
    (0, -1): [ys(f, y) for f, n in ((VX, 3), (VY, 2), (VZ, 3)) for y in range(n)],
    (1, 1): [some(VX, 7, 6, 2), some(VY, 6, 7), some(VY, 7, 7), some(CXY, 7, 7)],
    (-1, -1): [
        some(VX, 0, 0, 3),
        some(VX, 1, 0),
        some(VY, 0, 0, 2),
        some(VY, 1, 0),
        some(VY, 2, 0),
        some(VZ, 0, 0, 3),
        some(VZ, 1, 0),
        some(VZ, 2, 0),
    ]
    + [some(f, 0, 0) for f in (CXX, CYY, CZZ, CXY, CXZ, CYZ)],
    (-1, 1): [
        some(VX, 0, 6, 2),
        some(VY, 0, 6, 2),
        some(VY, 1, 7),
        some(VY, 2, 7),
        some(VZ, 0, 6, 2),
        some(CXY, 0, 7),
        some(CYZ, 0, 7),
    ],
    (1, -1): [
        some(VX, 7, 0, 3),
        some(VX, 6, 0),
        some(VY, 6, 0),
        some(VY, 7, 0),
        some(VZ, 6, 0),
        some(VZ, 7, 0),
        some(CXY, 7, 0),
        some(CXZ, 7, 0),
    ],
}


def joined(*tables):
    return {d: sum((t.get(d, []) for t in tables), []) for d in SIDES if any(d in t for t in tables)}


def rows_of(items):
    return -(-sum(item[4] for item in items) // 8) * 8


MESSAGES = []
for first in (True, False):
    MESSAGES.append(STRESS_SENT)
    faces_fixed = {d: FIXED_SENT[d] for d in FACES}
    MESSAGES.append(joined(BASE_SENT, faces_fixed) if first else BASE_SENT)
    corners_fixed = {d: FIXED_SENT[d] for d in CORNERS}
    MESSAGES.append(joined(VELOCITY_SENT, corners_fixed) if first else VELOCITY_SENT)

PLACES = {}
used = 0
for kind, table in enumerate(MESSAGES):
    for side, sent in table.items():
        PLACES[kind, side] = (used, rows_of(sent), len(PLACES))
        used += rows_of(sent)
BUFFER_ROWS = used
N_MESSAGES = len(PLACES)


def kernel(
    n_gx,
    n_gy,
    velocity_in,
    stress_in,
    memory_in,
    material_in,
    anelastic_in,
    zone_in,
    absorb_in,
    cells_in,
    moment_in,
    cohesion_table,
    friction_table,
    velocity_out,
    stress_out,
    memory_out,
    ext,
    sent,
    received,
    velocity,
    stress,
    memory,
    material,
    anelastic,
    zone,
    absorb,
    cells,
    moment,
    source,
    weight,
    centre,
    send_sem,
    recv_sem,
    in_sem,
    out_sem,
):
    gx, gy = lax.axis_index("gx"), lax.axis_index("gy")
    there = {}
    for dx, dy in SIDES:
        checks = []
        if dx:
            checks.append(gx > 0 if dx < 0 else gx < n_gx - 1)
        if dy:
            checks.append(gy > 0 if dy < 0 else gy < n_gy - 1)
        there[dx, dy] = checks[0] if len(checks) == 1 else jnp.logical_and(*checks)

    def device(d):
        return (gx + d[0], gy + d[1])

    barrier = pltpu.get_barrier_semaphore()
    for d in SIDES:

        @pl.when(there[d])
        def _():
            pl.semaphore_signal(barrier, 1, device_id=device(d), device_id_type=MESH)

    loads = []
    for k, (src, dst) in enumerate(
        (
            (stress_in, stress),
            (velocity_in, velocity),
            (memory_in, memory),
            (material_in, material),
            (anelastic_in, anelastic),
            (zone_in, zone),
            (absorb_in, absorb),
            (cells_in, cells),
            (moment_in, moment),
        )
    ):
        loads.append(pltpu.make_async_copy(src, dst, in_sem.at[k]))
        loads[-1].start()

    def at(item, d=(0, 0)):
        field, form, x, y, n = item
        start = row(x - 8 * d[0], y - 8 * d[1])
        return ext.at[field, pl.ds(start, n) if form == "B" else pl.ds(start, n, stride=PITCH), :]

    def copy_of(kind, d, sem_side):
        start, n, k = PLACES[kind, d]
        return pltpu.make_async_remote_copy(
            src_ref=sent.at[pl.ds(start, n)],
            dst_ref=received.at[pl.ds(start, n)],
            send_sem=send_sem.at[k],
            recv_sem=recv_sem.at[k],
            device_id=device(sem_side),
            device_id_type=MESH,
        )

    def pack(kind):
        for d, items in MESSAGES[kind].items():
            start = PLACES[kind, d][0]
            for item in items:
                sent[pl.ds(start, item[4]), :] = at(item)[...]
                start += item[4]

    def send(kind):
        for d in MESSAGES[kind]:

            @pl.when(there[d])
            def _():
                copy_of(kind, d, d).start()

    def receive(kind):
        for d, items in MESSAGES[kind].items():
            back = (-d[0], -d[1])

            @pl.when(there[back])
            def _():
                copy_of(kind, d, back).wait_recv()
                start = PLACES[kind, d][0]
                for item in items:
                    at(item, d)[...] = received[pl.ds(start, item[4]), :]
                    start += item[4]

    def outside(kind):
        for d, items in MESSAGES[kind].items():

            @pl.when(jnp.logical_not(there[-d[0], -d[1]]))
            def _():
                for item in items:
                    value = OPEN if item[0] == COH else 0.0
                    at(item, d)[...] = jnp.full((item[4], 128), value, jnp.float32)

    depth = lax.broadcasted_iota(jnp.int32, (8, 128), 1)

    def deeper(f, n):
        moved = pltpu.roll(f, (-n) % 128, 1)
        return jnp.where((depth < 128 - n) if n > 0 else (depth >= -n), moved, 0.0)

    def view(field, x, y, form):
        start = row(x, y)
        return ext[field, pl.ds(start, 8) if form == "B" else pl.ds(start, 8, stride=PITCH), :]

    def put(field, x, y, form, value):
        start = row(x, y)
        ext[field, pl.ds(start, 8) if form == "B" else pl.ds(start, 8, stride=PITCH), :] = value

    def along(field, x, y, form, axis, first):
        f = [
            view(field, x + (first + k if axis == 0 else 0), y + (first + k if axis == 1 else 0), form)
            for k in range(4)
        ]
        return NEAR * (f[2] - f[1]) + FAR * (f[3] - f[0])

    def forward(field, x, y, form, axis):
        return along(field, x, y, form, axis, -1)

    def backward(field, x, y, form, axis):
        return along(field, x, y, form, axis, -2)

    def forward_z(f):
        return NEAR * (deeper(f, 1) - f) + FAR * (deeper(f, 2) - deeper(f, -1))

    def backward_z(f):
        return NEAR * (f - deeper(f, -1)) + FAR * (deeper(f, 1) - deeper(f, -2))

    loads[0].wait()
    for x in range(8):
        for field, c in ((SXX, 0), (SXY, 3), (SXZ, 4), (SYY, 1), (SYZ, 5)):
            put(field, x, 0, "B", stress[c, x])
    pack(0)
    pl.semaphore_wait(barrier, sum(there[d].astype(jnp.int32) for d in SIDES))
    send(0)
    for kind in range(3):
        outside(kind)

    for load in loads[1:]:
        load.wait()
    place = cells[0]
    column = lax.broadcasted_iota(jnp.int32, (64, 128), 0) == (place // 128)
    spread = jnp.concatenate(
        [jnp.where(column, H * moment[0, 0, pl.ds(c, 1), :], 0.0) for c in range(6)], axis=0
    )
    at_depth = (lax.broadcasted_iota(jnp.int32, (128, 128), 0) == (place % 128)).astype(jnp.float32)
    source[...] = lax.dot_general(
        spread,
        at_depth,
        (((1,), (1,)), ((), ())),
        precision=lax.Precision.HIGHEST,
        preferred_element_type=jnp.float32,
    )
    for x in range(8):
        damping = jnp.where(absorb[x] == 1, SPONGE, 1.0)
        weight[0, x] = damping
        weight[1, x] = H * material[2, x] * damping
        grown = 1.0 - 0.5 * anelastic[1, x]
        weight[2, x] = grown
        put(PP, x, 0, "B", H * grown * material[0, x])
        put(QQ, x, 0, "B", H * grown * material[1, x])
        cohesion = jnp.zeros((8, 128), jnp.float32)
        friction = jnp.zeros((8, 128), jnp.float32)
        for z in range(ZONES):
            inside = zone[x] == z
            cohesion = jnp.where(inside, cohesion_table[z], cohesion)
            friction = jnp.where(inside, friction_table[z], friction)
        put(COH, x, 0, "B", cohesion)
        put(FRI, x, 0, "B", friction)

    ALL = (CXX, CYY, CZZ, CXY, CXZ, CYZ)
    F_STARTS = (-1, 1)

    for step in range(STEPS):
        kind = 3 * step
        if step:
            pack(kind)
            send(kind)
        for x in range(8):
            keep = 0.5 + 0.5 * anelastic[0, x]
            for c, field in enumerate(ALL):
                base = stress[c, x] + source[pl.ds(c * 64 + x * 8, 8), :] - keep * memory[c, x]
                put(field, x, 0, "B", base)
        pack(kind + 1)
        send(kind + 1)
        receive(kind)
        for x in range(8):
            rate_x = (
                forward(SXX, x, 0, "B", 0) + backward(SXY, x, 0, "B", 1) + backward_z(stress[4, x])
            )
            rate_y = (
                backward(SXY, x, 0, "B", 0) + forward(SYY, x, 0, "B", 1) + backward_z(stress[5, x])
            )
            rate_z = (
                backward(SXZ, x, 0, "B", 0) + backward(SYZ, x, 0, "B", 1) + forward_z(stress[2, x])
            )
            damping, push = weight[0, x], weight[1, x]
            for c, (field, rate) in enumerate(((VX, rate_x), (VY, rate_y), (VZ, rate_z))):
                new = velocity[c, x] * damping + push * rate
                velocity[c, x] = new
                put(field, x, 0, "B", new)
        pack(kind + 2)
        send(kind + 2)
        last = step == STEPS - 1
        if last:
            out_velocity = pltpu.make_async_copy(velocity, velocity_out, out_sem.at[0])
            out_velocity.start()
        receive(kind + 1)
        receive(kind + 2)

        def shear_xy(x, y, form):
            return forward(VX, x, y, form, 1) + forward(VY, x, y, form, 0)

        def shear_xz(x, y, form):
            return forward_z(view(VX, x, y, form)) + forward(VZ, x, y, form, 0)

        def shear_yz(x, y, form):
            return forward_z(view(VY, x, y, form)) + forward(VZ, x, y, form, 1)

        def normal(x, y, form):
            return (
                backward(VX, x, y, form, 0),
                backward(VY, x, y, form, 1),
                backward_z(view(VZ, x, y, form)),
            )

        def put_shear(field, x, y, form, value):
            put(field, x, y, form, value if field == TXY else value + deeper(value, -1))

        def keep_centre(k, x, y, form, trial):
            mean = (trial[0] + trial[1] + trial[2]) * (1.0 / 3.0)
            dev = [t - mean for t in trial]
            cohesion = view(COH, x, y, form)
            limit = jnp.maximum(cohesion - view(FRI, x, y, form) * mean, 0.25 * cohesion)
            centre[k, 0] = 0.5 * (dev[0] * dev[0] + dev[1] * dev[1] + dev[2] * dev[2])
            centre[k, 1] = limit
            if k < 8:
                centre[k, 2] = mean
                for c in range(3):
                    centre[k, 3 + c] = dev[c]

        for x in range(8):
            parts = normal(x, 0, "B")
            volume = parts[0] + parts[1] + parts[2]
            lame, modulus = H * material[0, x], H * material[1, x]
            spread_out = lame * volume
            rates = [spread_out + 2.0 * modulus * e for e in parts] + [
                modulus * e
                for e in (shear_xy(x, 0, "B"), shear_xz(x, 0, "B"), shear_yz(x, 0, "B"))
            ]
            grown, decay, share = weight[2, x], anelastic[0, x], anelastic[1, x]
            trial = []
            for c, field in enumerate(ALL):
                trial.append(view(field, x, 0, "B") + grown * rates[c])
                memory[c, x] = decay * memory[c, x] + share * rates[c]
            for c, field in ((3, TXY), (4, UXZ), (5, UYZ)):
                put_shear(field, x, 0, "B", trial[c])
                centre[x, 3 + c] = trial[c]
            keep_centre(x, x, 0, "B", trial[:3])
        if last:
            out_memory = pltpu.make_async_copy(memory, memory_out, out_sem.at[1])
            out_memory.start()
        beyond = [(8, 8, 0, "B")] + [(9 + k, x, 8, "F") for k, x in enumerate(F_STARTS)]
        for k, x, y, form in beyond:
            parts = normal(x, y, form)
            volume = parts[0] + parts[1] + parts[2]
            lame, modulus = view(PP, x, y, form), view(QQ, x, y, form)
            trial = [
                view(field, x, y, form) + lame * volume + 2.0 * modulus * e
                for field, e in zip(ALL, parts)
            ]
            keep_centre(k, x, y, form, trial)
            for field, base, e in (
                (TXY, CXY, shear_xy(x, y, form)),
                (UXZ, CXZ, shear_xz(x, y, form)),
                (UYZ, CYZ, shear_yz(x, y, form)),
            ):
                put_shear(field, x, y, form, view(base, x, y, form) + modulus * e)
        modulus = view(QQ, -1, 0, "B")
        put_shear(TXY, -1, 0, "B", view(CXY, -1, 0, "B") + modulus * shear_xy(-1, 0, "B"))
        put_shear(UXZ, -1, 0, "B", view(CXZ, -1, 0, "B") + modulus * shear_xz(-1, 0, "B"))
        for x in F_STARTS:
            modulus = view(QQ, x, -1, "F")
            put_shear(TXY, x, -1, "F", view(CXY, x, -1, "F") + modulus * shear_xy(x, -1, "F"))
            put_shear(UYZ, x, -1, "F", view(CYZ, x, -1, "F") + modulus * shear_yz(x, -1, "F"))

        for k, x, y, form in [(x, x, 0, "B") for x in range(8)] + beyond:
            mean_xy = 0.25 * (
                (view(TXY, x - 1, y - 1, form) + view(TXY, x - 1, y, form))
                + (view(TXY, x, y - 1, form) + view(TXY, x, y, form))
            )
            mean_xz = 0.25 * (view(UXZ, x - 1, y, form) + view(UXZ, x, y, form))
            mean_yz = 0.25 * (view(UYZ, x, y - 1, form) + view(UYZ, x, y, form))
            tau = jnp.sqrt(
                centre[k, 0] + mean_xy * mean_xy + mean_xz * mean_xz + mean_yz * mean_yz
            )
            ratio = jnp.minimum(1.0, centre[k, 1] / jnp.maximum(tau, 0.5))
            deficit = 1.0 - ratio
            put(DEF, x, y, form, deficit)
            put(DEZ, x, y, form, deficit + deeper(deficit, 1))
            if k < 8:
                centre[k, 1] = ratio

        for x in range(8):
            ratio, mean = centre[x, 1], centre[x, 2]
            new = [mean + ratio * centre[x, 3 + c] for c in range(3)]
            lack = [view(DEF, x + i, j, "B") for i in (0, 1) for j in (0, 1)]
            new.append((1.0 - 0.25 * ((lack[0] + lack[1]) + (lack[2] + lack[3]))) * centre[x, 6])
            here = view(DEZ, x, 0, "B")
            new.append((1.0 - 0.25 * (here + view(DEZ, x + 1, 0, "B"))) * centre[x, 7])
            new.append((1.0 - 0.25 * (here + view(DEZ, x, 1, "B"))) * centre[x, 8])
            for c in range(6):
                stress[c, x] = new[c]
            if not last:
                for field, c in ((SXX, 0), (SXY, 3), (SXZ, 4), (SYY, 1), (SYZ, 5)):
                    put(field, x, 0, "B", new[c])

    out_stress = pltpu.make_async_copy(stress, stress_out, out_sem.at[2])
    out_stress.start()
    for kind, table in enumerate(MESSAGES):
        for d in table:

            @pl.when(there[d])
            def _():
                copy_of(kind, d, d).wait_send()

    out_velocity.wait()
    out_memory.wait()
    out_stress.wait()


def shards(
    n_gx,
    n_gy,
    velocity,
    stress,
    memory,
    material,
    anelastic,
    zone_ids,
    absorb_mask,
    source_cells,
    source_moment,
    cohesion_table,
    friction_table,
):
    whole = pl.BlockSpec(memory_space=pl.ANY)
    table = pl.BlockSpec(memory_space=pltpu.SMEM)
    f32, i32 = jnp.float32, jnp.int32
    block = (8, 8, 128)
    return tuple(
        pl.pallas_call(
            functools.partial(kernel, n_gx, n_gy),
            out_shape=[
                jax.ShapeDtypeStruct((3, *block), f32),
                jax.ShapeDtypeStruct((6, *block), f32),
                jax.ShapeDtypeStruct((6, *block), f32),
            ],
            in_specs=[whole] * 9 + [table] * 2,
            out_specs=[whole] * 3,
            scratch_shapes=[
                pltpu.VMEM((FIELDS, SLABS * PITCH, 128), f32),
                pltpu.VMEM((BUFFER_ROWS, 128), f32),
                pltpu.VMEM((BUFFER_ROWS, 128), f32),
                pltpu.VMEM((3, *block), f32),
                pltpu.VMEM((6, *block), f32),
                pltpu.VMEM((6, *block), f32),
                pltpu.VMEM((3, *block), f32),
                pltpu.VMEM((2, *block), f32),
                pltpu.VMEM(block, i32),
                pltpu.VMEM(block, i32),
                pltpu.VMEM((1, 1, 128), i32),
                pltpu.VMEM((1, 1, 6, 128), f32),
                pltpu.VMEM((6 * 64, 128), f32),
                pltpu.VMEM((3, *block), f32),
                pltpu.VMEM((11, 9, 8, 128), f32),
                pltpu.SemaphoreType.DMA((N_MESSAGES,)),
                pltpu.SemaphoreType.DMA((N_MESSAGES,)),
                pltpu.SemaphoreType.DMA((9,)),
                pltpu.SemaphoreType.DMA((3,)),
            ],
            compiler_params=pltpu.CompilerParams(
                collective_id=0, has_side_effects=True, vmem_limit_bytes=48 * 2**20
            ),
            name="waves",
        )(
            velocity,
            stress,
            memory,
            material,
            anelastic,
            zone_ids,
            absorb_mask,
            source_cells,
            source_moment,
            cohesion_table,
            friction_table,
        )
    )


def solution(mesh):
    in_specs = (
        P(None, "gx", "gy", None),
        P(None, "gx", "gy", None),
        P(None, "gx", "gy", None),
        P(None, "gx", "gy", None),
        P(None, "gx", "gy", None),
        P("gx", "gy", None),
        P("gx", "gy", None),
        P("gx", "gy", None),
        P("gx", "gy", None, None),
        P(),
        P(),
    )
    out_specs = (P(None, "gx", "gy", None), P(None, "gx", "gy", None), P(None, "gx", "gy", None))
    body = functools.partial(shards, mesh.shape["gx"], mesh.shape["gy"])
    return jax.shard_map(body, mesh=mesh, in_specs=in_specs, out_specs=out_specs, check_vma=False)
```

```python
import functools

import jax
import jax.numpy as jnp
from jax import lax
from jax.experimental import pallas as pl
from jax.experimental.pallas import tpu as pltpu
from jax.sharding import PartitionSpec as P

MESH = pl.DeviceIdType.MESH
STEPS = 2
ZONES = 8
NEAR = 9.0 / 8.0
FAR = -1.0 / 24.0
H = 0.12
SPONGE = 0.92
OPEN = 1.0e9

SXX, SXY, SXZ, SYY, SYZ, VX, VY, VZ = range(8)
CXX, CYY, CZZ, CXY, CXZ, CYZ = range(8, 14)
PP, QQ, COH, FRI = range(14, 18)
TXY, UXZ, UYZ, DEF, DEZ = range(18, 23)
FIELDS = 23
SLABS = 14
PITCH = 16

FACES = ((-1, 0), (1, 0), (0, -1), (0, 1))
CORNERS = ((-1, -1), (-1, 1), (1, -1), (1, 1))
SIDES = FACES + CORNERS


def row(x, y):
    return (x + 3) * PITCH + (y + 4)


def xs(field, x):
    return (field, "B", x, 0, 8)


def ys(field, y):
    return (field, "F", 0, y, 8)


def some(field, x, y, n=1):
    return (field, "B", x, y, n)


STRESS_SENT = {
    (1, 0): [xs(SXX, 7), xs(SXY, 6), xs(SXY, 7), xs(SXZ, 6), xs(SXZ, 7)],
    (-1, 0): [xs(SXX, 0), xs(SXX, 1), xs(SXY, 0), xs(SXZ, 0)],
    (0, 1): [ys(SYY, 7), ys(SXY, 6), ys(SXY, 7), ys(SYZ, 6), ys(SYZ, 7)],
    (0, -1): [ys(SYY, 0), ys(SYY, 1), ys(SXY, 0), ys(SYZ, 0)],
}
BASE_SENT = {
    (1, 0): [xs(CXY, 7), xs(CXZ, 7)],
    (-1, 0): [xs(f, 0) for f in (CXX, CYY, CZZ, CXY, CXZ, CYZ)],
    (0, 1): [ys(CXY, 7), ys(CYZ, 7)],
    (0, -1): [ys(f, 0) for f in (CXX, CYY, CZZ, CXY, CXZ, CYZ)],
}
FIXED_SENT = {
    (1, 0): [xs(QQ, 7)],
    (-1, 0): [xs(f, 0) for f in (PP, QQ, COH, FRI)],
    (0, 1): [ys(QQ, 7)],
    (0, -1): [ys(f, 0) for f in (PP, QQ, COH, FRI)],
    (1, 1): [some(QQ, 7, 7)],
    (-1, -1): [some(f, 0, 0) for f in (PP, QQ, COH, FRI)],
    (-1, 1): [some(QQ, 0, 7)],
    (1, -1): [some(QQ, 7, 0)],
}
VELOCITY_SENT = {
    (1, 0): [xs(f, x) for f in (VX, VY, VZ) for x in (6, 7)],
    (-1, 0): [xs(f, x) for f, n in ((VX, 2), (VY, 3), (VZ, 3)) for x in range(n)],
    (0, 1): [ys(f, y) for f in (VX, VY, VZ) for y in (6, 7)],
    (0, -1): [ys(f, y) for f, n in ((VX, 3), (VY, 2), (VZ, 3)) for y in range(n)],
    (1, 1): [some(VX, 7, 6, 2), some(VY, 6, 7), some(VY, 7, 7), some(CXY, 7, 7)],
    (-1, -1): [
        some(VX, 0, 0, 3),
        some(VX, 1, 0),
        some(VY, 0, 0, 2),
        some(VY, 1, 0),
        some(VY, 2, 0),
        some(VZ, 0, 0, 3),
        some(VZ, 1, 0),
        some(VZ, 2, 0),
    ]
    + [some(f, 0, 0) for f in (CXX, CYY, CZZ, CXY, CXZ, CYZ)],
    (-1, 1): [
        some(VX, 0, 6, 2),
        some(VY, 0, 6, 2),
        some(VY, 1, 7),
        some(VY, 2, 7),
        some(VZ, 0, 6, 2),
        some(CXY, 0, 7),
        some(CYZ, 0, 7),
    ],
    (1, -1): [
        some(VX, 7, 0, 3),
        some(VX, 6, 0),
        some(VY, 6, 0),
        some(VY, 7, 0),
        some(VZ, 6, 0),
        some(VZ, 7, 0),
        some(CXY, 7, 0),
        some(CXZ, 7, 0),
    ],
}


def joined(*tables):
    return {d: sum((t.get(d, []) for t in tables), []) for d in SIDES if any(d in t for t in tables)}


def rows_of(items):
    return -(-sum(item[4] for item in items) // 8) * 8


MESSAGES = []
for first in (True, False):
    MESSAGES.append(STRESS_SENT)
    faces_fixed = {d: FIXED_SENT[d] for d in FACES}
    MESSAGES.append(joined(BASE_SENT, faces_fixed) if first else BASE_SENT)
    corners_fixed = {d: FIXED_SENT[d] for d in CORNERS}
    MESSAGES.append(joined(VELOCITY_SENT, corners_fixed) if first else VELOCITY_SENT)

PLACES = {}
used = 0
for kind, table in enumerate(MESSAGES):
    for side, sent in table.items():
        PLACES[kind, side] = (used, rows_of(sent), len(PLACES))
        used += rows_of(sent)
BUFFER_ROWS = used
N_MESSAGES = len(PLACES)


def kernel(
    n_gx,
    n_gy,
    velocity_in,
    stress_in,
    memory_in,
    material_in,
    anelastic_in,
    zone_in,
    absorb_in,
    cells_in,
    moment_in,
    cohesion_in,
    friction_in,
    velocity,
    stress,
    memory,
    ext,
    sent,
    received,
    material,
    anelastic,
    zone,
    absorb,
    cells,
    moment,
    cohesion_table,
    friction_table,
    source,
    weight,
    centre,
    send_sem,
    recv_sem,
    in_sem,
):
    gx, gy = lax.axis_index("gx"), lax.axis_index("gy")
    there = {}
    for dx, dy in SIDES:
        checks = []
        if dx:
            checks.append(gx > 0 if dx < 0 else gx < n_gx - 1)
        if dy:
            checks.append(gy > 0 if dy < 0 else gy < n_gy - 1)
        there[dx, dy] = checks[0] if len(checks) == 1 else jnp.logical_and(*checks)

    def device(d):
        return (gx + d[0], gy + d[1])

    barrier = pltpu.get_barrier_semaphore()
    for d in SIDES:

        @pl.when(there[d])
        def _():
            pl.semaphore_signal(barrier, 1, device_id=device(d), device_id_type=MESH)

    loads = []
    for k, (src, dst) in enumerate(
        (
            (stress_in, stress),
            (velocity_in, velocity),
            (memory_in, memory),
            (material_in, material),
            (anelastic_in, anelastic),
            (zone_in, zone),
            (absorb_in, absorb),
            (cells_in, cells),
            (moment_in, moment),
            (cohesion_in, cohesion_table),
            (friction_in, friction_table),
        )
    ):
        loads.append(pltpu.make_async_copy(src, dst, in_sem.at[k]))
        loads[-1].start()

    def at(item, d=(0, 0)):
        field, form, x, y, n = item
        start = row(x - 8 * d[0], y - 8 * d[1])
        return ext.at[field, pl.ds(start, n) if form == "B" else pl.ds(start, n, stride=PITCH), :]

    def copy_of(kind, d, sem_side):
        start, n, k = PLACES[kind, d]
        return pltpu.make_async_remote_copy(
            src_ref=sent.at[pl.ds(start, n)],
            dst_ref=received.at[pl.ds(start, n)],
            send_sem=send_sem.at[k],
            recv_sem=recv_sem.at[k],
            device_id=device(sem_side),
            device_id_type=MESH,
        )

    def pack(kind):
        for d, items in MESSAGES[kind].items():
            start = PLACES[kind, d][0]
            for item in items:
                sent[pl.ds(start, item[4]), :] = at(item)[...]
                start += item[4]

    def send(kind):
        for d in MESSAGES[kind]:

            @pl.when(there[d])
            def _():
                copy_of(kind, d, d).start()

    def receive(kind):
        for d, items in MESSAGES[kind].items():
            back = (-d[0], -d[1])

            @pl.when(there[back])
            def _():
                copy_of(kind, d, back).wait_recv()
                start = PLACES[kind, d][0]
                for item in items:
                    at(item, d)[...] = received[pl.ds(start, item[4]), :]
                    start += item[4]

    def outside(kind):
        for d, items in MESSAGES[kind].items():

            @pl.when(jnp.logical_not(there[-d[0], -d[1]]))
            def _():
                for item in items:
                    value = OPEN if item[0] == COH else 0.0
                    at(item, d)[...] = jnp.full((item[4], 128), value, jnp.float32)

    depth = lax.broadcasted_iota(jnp.int32, (8, 128), 1)

    def deeper(f, n):
        moved = pltpu.roll(f, (-n) % 128, 1)
        return jnp.where((depth < 128 - n) if n > 0 else (depth >= -n), moved, 0.0)

    def view(field, x, y, form):
        start = row(x, y)
        return ext[field, pl.ds(start, 8) if form == "B" else pl.ds(start, 8, stride=PITCH), :]

    def put(field, x, y, form, value):
        start = row(x, y)
        ext[field, pl.ds(start, 8) if form == "B" else pl.ds(start, 8, stride=PITCH), :] = value

    def along(field, x, y, form, axis, first):
        f = [
            view(field, x + (first + k if axis == 0 else 0), y + (first + k if axis == 1 else 0), form)
            for k in range(4)
        ]
        return NEAR * (f[2] - f[1]) + FAR * (f[3] - f[0])

    def forward(field, x, y, form, axis):
        return along(field, x, y, form, axis, -1)

    def backward(field, x, y, form, axis):
        return along(field, x, y, form, axis, -2)

    def forward_z(f):
        return NEAR * (deeper(f, 1) - f) + FAR * (deeper(f, 2) - deeper(f, -1))

    def backward_z(f):
        return NEAR * (f - deeper(f, -1)) + FAR * (deeper(f, 1) - deeper(f, -2))

    loads[0].wait()
    for x in range(8):
        for field, c in ((SXX, 0), (SXY, 3), (SXZ, 4), (SYY, 1), (SYZ, 5)):
            put(field, x, 0, "B", stress[c, x])
    pack(0)
    pl.semaphore_wait(barrier, sum(there[d].astype(jnp.int32) for d in SIDES))
    send(0)
    for kind in range(3):
        outside(kind)

    for load in loads[1:]:
        load.wait()
    place = cells[0]
    column = lax.broadcasted_iota(jnp.int32, (64, 128), 0) == (place // 128)
    spread = jnp.concatenate(
        [jnp.where(column, H * moment[0, c], 0.0) for c in range(6)], axis=0
    )
    at_depth = (lax.broadcasted_iota(jnp.int32, (128, 128), 0) == (place % 128)).astype(jnp.float32)
    source[...] = lax.dot_general(
        spread,
        at_depth,
        (((1,), (1,)), ((), ())),
        precision=lax.Precision.HIGHEST,
        preferred_element_type=jnp.float32,
    )
    for x in range(8):
        damping = jnp.where(absorb[x] == 1, SPONGE, 1.0)
        weight[0, x] = damping
        weight[1, x] = H * material[2, x] * damping
        grown = 1.0 - 0.5 * anelastic[1, x]
        weight[2, x] = grown
        put(PP, x, 0, "B", H * grown * material[0, x])
        put(QQ, x, 0, "B", H * grown * material[1, x])
        cohesion = jnp.zeros((8, 128), jnp.float32)
        friction = jnp.zeros((8, 128), jnp.float32)
        for z in range(ZONES):
            inside = zone[x] == z
            cohesion = jnp.where(inside, cohesion_table[z], cohesion)
            friction = jnp.where(inside, friction_table[z], friction)
        put(COH, x, 0, "B", cohesion)
        put(FRI, x, 0, "B", friction)

    ALL = (CXX, CYY, CZZ, CXY, CXZ, CYZ)
    F_STARTS = (-1, 1)

    for step in range(STEPS):
        kind = 3 * step
        if step:
            pack(kind)
            send(kind)
        for x in range(8):
            keep = 0.5 + 0.5 * anelastic[0, x]
            for c, field in enumerate(ALL):
                base = stress[c, x] + source[pl.ds(c * 64 + x * 8, 8), :] - keep * memory[c, x]
                put(field, x, 0, "B", base)
        pack(kind + 1)
        send(kind + 1)
        receive(kind)
        for x in range(8):
            rate_x = (
                forward(SXX, x, 0, "B", 0) + backward(SXY, x, 0, "B", 1) + backward_z(stress[4, x])
            )
            rate_y = (
                backward(SXY, x, 0, "B", 0) + forward(SYY, x, 0, "B", 1) + backward_z(stress[5, x])
            )
            rate_z = (
                backward(SXZ, x, 0, "B", 0) + backward(SYZ, x, 0, "B", 1) + forward_z(stress[2, x])
            )
            damping, push = weight[0, x], weight[1, x]
            for c, (field, rate) in enumerate(((VX, rate_x), (VY, rate_y), (VZ, rate_z))):
                new = velocity[c, x] * damping + push * rate
                velocity[c, x] = new
                put(field, x, 0, "B", new)
        pack(kind + 2)
        send(kind + 2)
        last = step == STEPS - 1
        receive(kind + 1)
        receive(kind + 2)

        def shear_xy(x, y, form):
            return forward(VX, x, y, form, 1) + forward(VY, x, y, form, 0)

        def shear_xz(x, y, form):
            return forward_z(view(VX, x, y, form)) + forward(VZ, x, y, form, 0)

        def shear_yz(x, y, form):
            return forward_z(view(VY, x, y, form)) + forward(VZ, x, y, form, 1)

        def normal(x, y, form):
            return (
                backward(VX, x, y, form, 0),
                backward(VY, x, y, form, 1),
                backward_z(view(VZ, x, y, form)),
            )

        def put_shear(field, x, y, form, value):
            put(field, x, y, form, value if field == TXY else value + deeper(value, -1))

        def keep_centre(k, x, y, form, trial):
            mean = (trial[0] + trial[1] + trial[2]) * (1.0 / 3.0)
            dev = [t - mean for t in trial]
            cohesion = view(COH, x, y, form)
            limit = jnp.maximum(cohesion - view(FRI, x, y, form) * mean, 0.25 * cohesion)
            centre[k, 0] = 0.5 * (dev[0] * dev[0] + dev[1] * dev[1] + dev[2] * dev[2])
            centre[k, 1] = limit
            if k < 8:
                centre[k, 2] = mean
                for c in range(3):
                    centre[k, 3 + c] = dev[c]

        for x in range(8):
            parts = normal(x, 0, "B")
            volume = parts[0] + parts[1] + parts[2]
            lame, modulus = H * material[0, x], H * material[1, x]
            spread_out = lame * volume
            rates = [spread_out + 2.0 * modulus * e for e in parts] + [
                modulus * e
                for e in (shear_xy(x, 0, "B"), shear_xz(x, 0, "B"), shear_yz(x, 0, "B"))
            ]
            grown, decay, share = weight[2, x], anelastic[0, x], anelastic[1, x]
            trial = []
            for c, field in enumerate(ALL):
                trial.append(view(field, x, 0, "B") + grown * rates[c])
                memory[c, x] = decay * memory[c, x] + share * rates[c]
            for c, field in ((3, TXY), (4, UXZ), (5, UYZ)):
                put_shear(field, x, 0, "B", trial[c])
                centre[x, 3 + c] = trial[c]
            keep_centre(x, x, 0, "B", trial[:3])
        beyond = [(8, 8, 0, "B")] + [(9 + k, x, 8, "F") for k, x in enumerate(F_STARTS)]
        for k, x, y, form in beyond:
            parts = normal(x, y, form)
            volume = parts[0] + parts[1] + parts[2]
            lame, modulus = view(PP, x, y, form), view(QQ, x, y, form)
            trial = [
                view(field, x, y, form) + lame * volume + 2.0 * modulus * e
                for field, e in zip(ALL, parts)
            ]
            keep_centre(k, x, y, form, trial)
            for field, base, e in (
                (TXY, CXY, shear_xy(x, y, form)),
                (UXZ, CXZ, shear_xz(x, y, form)),
                (UYZ, CYZ, shear_yz(x, y, form)),
            ):
                put_shear(field, x, y, form, view(base, x, y, form) + modulus * e)
        modulus = view(QQ, -1, 0, "B")
        put_shear(TXY, -1, 0, "B", view(CXY, -1, 0, "B") + modulus * shear_xy(-1, 0, "B"))
        put_shear(UXZ, -1, 0, "B", view(CXZ, -1, 0, "B") + modulus * shear_xz(-1, 0, "B"))
        for x in F_STARTS:
            modulus = view(QQ, x, -1, "F")
            put_shear(TXY, x, -1, "F", view(CXY, x, -1, "F") + modulus * shear_xy(x, -1, "F"))
            put_shear(UYZ, x, -1, "F", view(CYZ, x, -1, "F") + modulus * shear_yz(x, -1, "F"))

        for k, x, y, form in [(x, x, 0, "B") for x in range(8)] + beyond:
            mean_xy = 0.25 * (
                (view(TXY, x - 1, y - 1, form) + view(TXY, x - 1, y, form))
                + (view(TXY, x, y - 1, form) + view(TXY, x, y, form))
            )
            mean_xz = 0.25 * (view(UXZ, x - 1, y, form) + view(UXZ, x, y, form))
            mean_yz = 0.25 * (view(UYZ, x, y - 1, form) + view(UYZ, x, y, form))
            tau = jnp.sqrt(
                centre[k, 0] + mean_xy * mean_xy + mean_xz * mean_xz + mean_yz * mean_yz
            )
            ratio = jnp.minimum(1.0, centre[k, 1] / jnp.maximum(tau, 0.5))
            deficit = 1.0 - ratio
            put(DEF, x, y, form, deficit)
            put(DEZ, x, y, form, deficit + deeper(deficit, 1))
            if k < 8:
                centre[k, 1] = ratio

        for x in range(8):
            ratio, mean = centre[x, 1], centre[x, 2]
            new = [mean + ratio * centre[x, 3 + c] for c in range(3)]
            lack = [view(DEF, x + i, j, "B") for i in (0, 1) for j in (0, 1)]
            new.append((1.0 - 0.25 * ((lack[0] + lack[1]) + (lack[2] + lack[3]))) * centre[x, 6])
            here = view(DEZ, x, 0, "B")
            new.append((1.0 - 0.25 * (here + view(DEZ, x + 1, 0, "B"))) * centre[x, 7])
            new.append((1.0 - 0.25 * (here + view(DEZ, x, 1, "B"))) * centre[x, 8])
            for c in range(6):
                stress[c, x] = new[c]
            if not last:
                for field, c in ((SXX, 0), (SXY, 3), (SXZ, 4), (SYY, 1), (SYZ, 5)):
                    put(field, x, 0, "B", new[c])

    for kind, table in enumerate(MESSAGES):
        for d in table:

            @pl.when(there[d])
            def _():
                copy_of(kind, d, d).wait_send()


def hand_over(*refs):
    n = (len(refs) - 1) // 2
    copies = [pltpu.make_async_copy(refs[k], refs[n + k], refs[-1].at[k]) for k in range(n)]
    for copy in copies:
        copy.start()
    for copy in copies:
        copy.wait()


def shards(
    n_gx,
    n_gy,
    velocity,
    stress,
    memory,
    material,
    anelastic,
    zone_ids,
    absorb_mask,
    source_cells,
    source_moment,
    cohesion_table,
    friction_table,
):
    far = pl.BlockSpec(memory_space=pl.ANY)
    near = pl.BlockSpec(memory_space=pltpu.VMEM)
    f32, i32 = jnp.float32, jnp.int32
    block = (8, 8, 128)
    operands = (
        velocity,
        stress,
        memory,
        material,
        anelastic,
        zone_ids,
        absorb_mask,
        source_cells,
        jnp.swapaxes(source_moment, 1, 2),
        cohesion_table,
        friction_table,
    )
    results = pl.pallas_call(
        functools.partial(kernel, n_gx, n_gy),
        out_shape=[pltpu.VMEM((n, *block), f32) for n in (3, 6, 6)],
        in_specs=[far] * 11,
        out_specs=[near] * 3,
        scratch_shapes=[
            pltpu.VMEM((FIELDS, SLABS * PITCH, 128), f32),
            pltpu.VMEM((BUFFER_ROWS, 128), f32),
            pltpu.VMEM((BUFFER_ROWS, 128), f32),
            pltpu.VMEM((3, *block), f32),
            pltpu.VMEM((2, *block), f32),
            pltpu.VMEM(block, i32),
            pltpu.VMEM(block, i32),
            pltpu.VMEM((1, 1, 128), i32),
            pltpu.VMEM((1, 6, 1, 128), f32),
            pltpu.SMEM((ZONES,), f32),
            pltpu.SMEM((ZONES,), f32),
            pltpu.VMEM((6 * 64, 128), f32),
            pltpu.VMEM((3, *block), f32),
            pltpu.VMEM((11, 9, 8, 128), f32),
            pltpu.SemaphoreType.DMA((N_MESSAGES,)),
            pltpu.SemaphoreType.DMA((N_MESSAGES,)),
            pltpu.SemaphoreType.DMA((11,)),
        ],
        compiler_params=pltpu.CompilerParams(
            collective_id=0, has_side_effects=True, vmem_limit_bytes=32 * 2**20
        ),
        name="waves",
    )(*[pltpu.with_memory_space_constraint(x, pltpu.HBM) for x in operands])
    return tuple(
        pl.pallas_call(
            hand_over,
            out_shape=[jax.ShapeDtypeStruct(r.shape, r.dtype) for r in results],
            in_specs=[near] * 3,
            out_specs=[far] * 3,
            scratch_shapes=[pltpu.SemaphoreType.DMA((3,))],
            name="results",
        )(*[pltpu.with_memory_space_constraint(r, pltpu.VMEM) for r in results])
    )


def solution(mesh):
    in_specs = (
        P(None, "gx", "gy", None),
        P(None, "gx", "gy", None),
        P(None, "gx", "gy", None),
        P(None, "gx", "gy", None),
        P(None, "gx", "gy", None),
        P("gx", "gy", None),
        P("gx", "gy", None),
        P("gx", "gy", None),
        P("gx", "gy", None, None),
        P(),
        P(),
    )
    out_specs = (P(None, "gx", "gy", None), P(None, "gx", "gy", None), P(None, "gx", "gy", None))
    body = functools.partial(shards, mesh.shape["gx"], mesh.shape["gy"])
    return jax.shard_map(body, mesh=mesh, in_specs=in_specs, out_specs=out_specs, check_vma=False)
```

```python
import functools

import jax
import jax.numpy as jnp
from jax import lax
from jax.experimental import pallas as pl
from jax.experimental.pallas import tpu as pltpu
from jax.sharding import PartitionSpec as P

MESH = pl.DeviceIdType.MESH
STEPS = 2
ZONES = 8
NEAR = 9.0 / 8.0
FAR = -1.0 / 24.0
H = 0.12
SPONGE = 0.92
OPEN = 1.0e9

SXX, SXY, SXZ, SYY, SYZ, VX, VY, VZ, RX, RY, RZ = range(11)
CXX, CYY, CZZ, CXY, CXZ, CYZ = range(11, 17)
PP, QQ, COH, FRI, PUSH = range(17, 22)
TXY, UXZ, UYZ, DEF, DEZ = range(22, 27)
FIELDS = 27
SLABS = 14
PITCH = 16

FACES = ((-1, 0), (1, 0), (0, -1), (0, 1))
CORNERS = ((-1, -1), (-1, 1), (1, -1), (1, 1))
SIDES = FACES + CORNERS


def row(x, y):
    return (x + 3) * PITCH + (y + 4)


def xs(field, x):
    return (field, "B", x, 0, 8)


def ys(field, y):
    return (field, "F", 0, y, 8)


def some(field, x, y, n=1):
    return (field, "B", x, y, n)


def boxes(*parts):
    return [some(f, x, y, n) for f, x, y, n in parts]


def rows_x(field, *at):
    return [xs(field, x) for x in at]


def rows_y(field, *at):
    return [ys(field, y) for y in at]


NORMAL_AND_SHEAR = (CXX, CYY, CZZ, CXY, CXZ, CYZ)

EACH_STEP = {
    (1, 0): rows_x(VX, 6, 7) + rows_x(VY, 6, 7) + rows_x(VZ, 6, 7)
    + rows_x(RX, 8) + rows_x(RY, 8, 9) + rows_x(RZ, 8, 9) + rows_x(CXY, 7) + rows_x(CXZ, 7)
    + boxes((RX, 7, 8, 2), (RX, 6, 8, 1), (RY, 6, 8, 1), (RY, 7, 8, 1), (RZ, 6, 8, 1), (RZ, 7, 8, 1))
    + boxes((RX, 7, -1, 1), (RY, 6, -1, 1), (RY, 7, -1, 1)),
    (-1, 0): rows_x(VX, 0, 1) + rows_x(VY, 0, 1, 2) + rows_x(VZ, 0, 1, 2)
    + rows_x(RX, -2, -1) + rows_x(RY, -1) + rows_x(RZ, -1)
    + [xs(f, 0) for f in NORMAL_AND_SHEAR]
    + boxes((RX, 0, 8, 2), (RX, 1, 8, 1), (RY, 0, 8, 1), (RY, 1, 8, 1), (RY, 2, 8, 1))
    + boxes((RZ, 0, 8, 2), (RZ, 1, 8, 1), (RZ, 2, 8, 1))
    + boxes((RX, 0, -1, 1), (RY, 0, -2, 2), (RY, 1, -1, 1), (RY, 2, -1, 1), (RZ, 0, -1, 1)),
    (0, 1): rows_y(VX, 6, 7) + rows_y(VY, 6, 7) + rows_y(VZ, 6, 7)
    + rows_y(RY, 8) + rows_y(RX, 8, 9) + rows_y(RZ, 8, 9) + rows_y(CXY, 7) + rows_y(CYZ, 7)
    + boxes((RX, 8, 6, 2), (RY, 8, 6, 2), (RY, 9, 7, 1), (RZ, 8, 6, 2))
    + boxes((RX, -1, 6, 2), (RY, -1, 7, 1)),
    (0, -1): rows_y(VY, 0, 1) + rows_y(VX, 0, 1, 2) + rows_y(VZ, 0, 1, 2)
    + rows_y(RY, -2, -1) + rows_y(RX, -1) + rows_y(RZ, -1)
    + [ys(f, 0) for f in NORMAL_AND_SHEAR]
    + boxes((RX, 8, 0, 3), (RY, 8, 0, 2), (RY, 9, 0, 1), (RZ, 8, 0, 3), (RZ, 9, 0, 1))
    + boxes((RX, -1, 0, 3), (RX, -2, 0, 1), (RY, -1, 0, 1), (RZ, -1, 0, 1)),
    (1, 1): boxes((VX, 7, 6, 2), (VY, 6, 7, 1), (VY, 7, 7, 1), (CXY, 7, 7, 1))
    + boxes((RX, 6, 8, 2), (RX, 7, 8, 2), (RY, 6, 8, 1), (RY, 7, 8, 1), (RZ, 6, 8, 2), (RZ, 7, 8, 2))
    + boxes((RX, 8, 6, 2), (RY, 8, 6, 2), (RY, 9, 6, 2), (RZ, 8, 6, 2), (RZ, 9, 6, 2)),
    (-1, -1): boxes((VX, 0, 0, 3), (VX, 1, 0, 1), (VY, 0, 0, 2), (VY, 1, 0, 1), (VY, 2, 0, 1))
    + boxes((VZ, 0, 0, 3), (VZ, 1, 0, 1), (VZ, 2, 0, 1))
    + [some(f, 0, 0) for f in NORMAL_AND_SHEAR]
    + boxes((RX, 0, -1, 1), (RX, 1, -1, 1), (RY, 0, -2, 2), (RY, 1, -2, 2), (RY, 2, -2, 2))
    + boxes((RZ, 0, -1, 1), (RZ, 1, -1, 1), (RZ, 2, -1, 1))
    + boxes((RX, -2, 0, 3), (RX, -1, 0, 3), (RY, -1, 0, 2), (RZ, -1, 0, 3)),
    (-1, 1): boxes((VX, 0, 6, 2), (VY, 0, 6, 2), (VY, 1, 7, 1), (VY, 2, 7, 1), (VZ, 0, 6, 2))
    + boxes((CXY, 0, 7, 1), (CYZ, 0, 7, 1))
    + boxes((RX, 0, 8, 2), (RX, 1, 8, 2), (RY, 0, 8, 1), (RY, 1, 8, 1), (RY, 2, 8, 1))
    + boxes((RZ, 0, 8, 2), (RZ, 1, 8, 2), (RZ, 2, 8, 2))
    + boxes((RX, -2, 6, 2), (RX, -1, 6, 2), (RY, -1, 6, 2), (RZ, -1, 6, 2)),
    (1, -1): boxes((VX, 7, 0, 3), (VX, 6, 0, 1), (VY, 6, 0, 1), (VY, 7, 0, 1), (VZ, 6, 0, 1), (VZ, 7, 0, 1))
    + boxes((CXY, 7, 0, 1), (CXZ, 7, 0, 1))
    + boxes((RX, 6, -1, 1), (RX, 7, -1, 1), (RY, 6, -2, 2), (RY, 7, -2, 2), (RZ, 6, -1, 1), (RZ, 7, -1, 1))
    + boxes((RX, 8, 0, 3), (RY, 8, 0, 2), (RY, 9, 0, 2), (RZ, 8, 0, 3), (RZ, 9, 0, 3)),
}
ONCE = {
    (1, 0): rows_x(QQ, 7) + rows_x(PUSH, 6, 7),
    (-1, 0): [xs(f, 0) for f in (PP, QQ, COH, FRI)] + rows_x(PUSH, 0, 1, 2),
    (0, 1): rows_y(QQ, 7) + rows_y(PUSH, 6, 7),
    (0, -1): [ys(f, 0) for f in (PP, QQ, COH, FRI)] + rows_y(PUSH, 0, 1, 2),
    (1, 1): boxes((QQ, 7, 7, 1), (PUSH, 7, 6, 2), (PUSH, 6, 7, 1)),
    (-1, -1): [some(f, 0, 0) for f in (PP, QQ, COH, FRI)]
    + boxes((PUSH, 0, 0, 3), (PUSH, 1, 0, 1), (PUSH, 2, 0, 1)),
    (-1, 1): boxes((QQ, 0, 7, 1), (PUSH, 0, 6, 2), (PUSH, 1, 7, 1), (PUSH, 2, 7, 1)),
    (1, -1): boxes((QQ, 7, 0, 1), (PUSH, 7, 0, 3), (PUSH, 6, 0, 1)),
}


def rows_of(items):
    return -(-sum(item[4] for item in items) // 8) * 8


MESSAGES = [{d: ONCE[d] + EACH_STEP[d] for d in SIDES}, EACH_STEP]

PLACES = {}
used = 0
for kind, table in enumerate(MESSAGES):
    for side, sent in table.items():
        PLACES[kind, side] = (used, rows_of(sent), len(PLACES))
        used += rows_of(sent)
BUFFER_ROWS = used
N_MESSAGES = len(PLACES)


def kernel(
    n_gx,
    n_gy,
    velocity_in,
    stress_in,
    memory_in,
    material_in,
    anelastic_in,
    zone_in,
    absorb_in,
    cells_in,
    moment_in,
    cohesion_in,
    friction_in,
    velocity,
    stress,
    memory,
    ext,
    sent,
    received,
    material,
    anelastic,
    zone,
    absorb,
    cells,
    moment,
    cohesion_table,
    friction_table,
    source,
    weight,
    centre,
    send_sem,
    recv_sem,
    in_sem,
):
    gx, gy = lax.axis_index("gx"), lax.axis_index("gy")
    there = {}
    for dx, dy in SIDES:
        checks = []
        if dx:
            checks.append(gx > 0 if dx < 0 else gx < n_gx - 1)
        if dy:
            checks.append(gy > 0 if dy < 0 else gy < n_gy - 1)
        there[dx, dy] = checks[0] if len(checks) == 1 else jnp.logical_and(*checks)

    def device(d):
        return (gx + d[0], gy + d[1])

    barrier = pltpu.get_barrier_semaphore()
    for d in SIDES:

        @pl.when(there[d])
        def _():
            pl.semaphore_signal(barrier, 1, device_id=device(d), device_id_type=MESH)

    loads = []
    for k, (src, dst) in enumerate(
        (
            (stress_in, stress),
            (velocity_in, velocity),
            (memory_in, memory),
            (material_in, material),
            (anelastic_in, anelastic),
            (zone_in, zone),
            (absorb_in, absorb),
            (cells_in, cells),
            (moment_in, moment),
            (cohesion_in, cohesion_table),
            (friction_in, friction_table),
        )
    ):
        loads.append(pltpu.make_async_copy(src, dst, in_sem.at[k]))
        loads[-1].start()

    def spot(field, form, x, y, n):
        start = row(x, y)
        return ext.at[field, pl.ds(start, n) if form == "B" else pl.ds(start, n, stride=PITCH), :]

    def at(item):
        return spot(*item)

    def landed(item, d):
        field, form, x, y, n = item
        return (field, form, x - 8 * d[0], y - 8 * d[1], n)

    def copy_of(kind, d, sem_side):
        start, n, k = PLACES[kind, d]
        return pltpu.make_async_remote_copy(
            src_ref=sent.at[pl.ds(start, n)],
            dst_ref=received.at[pl.ds(start, n)],
            send_sem=send_sem.at[k],
            recv_sem=recv_sem.at[k],
            device_id=device(sem_side),
            device_id_type=MESH,
        )

    def pack(kind):
        for d, items in MESSAGES[kind].items():
            start = PLACES[kind, d][0]
            for item in items:
                sent[pl.ds(start, item[4]), :] = at(item)[...]
                start += item[4]

    def send(kind):
        for d in MESSAGES[kind]:

            @pl.when(there[d])
            def _():
                copy_of(kind, d, d).start()

    def receive(kind):
        for d, items in MESSAGES[kind].items():
            back = (-d[0], -d[1])

            @pl.when(there[back])
            def _():
                copy_of(kind, d, back).wait_recv()
                start = PLACES[kind, d][0]
                for item in items:
                    value = received[pl.ds(start, item[4]), :]
                    start += item[4]
                    field, form, x, y, n = landed(item, d)
                    if field in (RX, RY, RZ) and 0 <= x < 8 and 0 <= y < 8:
                        mine = spot(field - RX + VX, form, x, y, n)
                        mine[...] = mine[...] + spot(PUSH, form, x, y, n)[...] * value
                    elif field in (RX, RY, RZ):
                        rates = spot(field, form, x, y, n)
                        rates[...] = rates[...] + value
                    else:
                        spot(field, form, x, y, n)[...] = value

    def outside(kind):
        for d, items in MESSAGES[kind].items():

            @pl.when(jnp.logical_not(there[-d[0], -d[1]]))
            def _():
                for item in items:
                    if item[0] not in (RX, RY, RZ):
                        value = OPEN if item[0] == COH else 0.0
                        spot(*landed(item, d))[...] = jnp.full((item[4], 128), value, jnp.float32)

    depth = lax.broadcasted_iota(jnp.int32, (8, 128), 1)

    def deeper(f, n):
        moved = pltpu.roll(f, (-n) % 128, 1)
        return jnp.where((depth < 128 - n) if n > 0 else (depth >= -n), moved, 0.0)

    def view(field, x, y, form):
        start = row(x, y)
        return ext[field, pl.ds(start, 8) if form == "B" else pl.ds(start, 8, stride=PITCH), :]

    def put(field, x, y, form, value):
        start = row(x, y)
        ext[field, pl.ds(start, 8) if form == "B" else pl.ds(start, 8, stride=PITCH), :] = value

    def along(field, x, y, form, axis, first):
        f = [
            view(field, x + (first + k if axis == 0 else 0), y + (first + k if axis == 1 else 0), form)
            for k in range(4)
        ]
        return NEAR * (f[2] - f[1]) + FAR * (f[3] - f[0])

    def forward(field, x, y, form, axis):
        return along(field, x, y, form, axis, -1)

    def backward(field, x, y, form, axis):
        return along(field, x, y, form, axis, -2)

    def forward_z(f):
        return NEAR * (deeper(f, 1) - f) + FAR * (deeper(f, 2) - deeper(f, -1))

    def backward_z(f):
        return NEAR * (f - deeper(f, -1)) + FAR * (deeper(f, 1) - deeper(f, -2))

    nothing = jnp.zeros((8, 128), jnp.float32)
    for field in (SXX, SXY, SXZ, SYY, SYZ):
        for x in (-2, -1, 8, 9):
            put(field, x, -4, "B", nothing)
            put(field, x, 4, "B", nothing)
        for y in (-2, -1, 8, 9):
            put(field, 0, y, "F", nothing)
    outside(0)
    loads[0].wait()
    for x in range(8):
        for field, c in ((SXX, 0), (SXY, 3), (SXZ, 4), (SYY, 1), (SYZ, 5)):
            put(field, x, 0, "B", stress[c, x])

    for k, load in enumerate(loads):
        if k:
            load.wait()
    place = cells[0]
    column = lax.broadcasted_iota(jnp.int32, (64, 128), 0) == (place // 128)
    spread = jnp.concatenate(
        [jnp.where(column, H * moment[0, c], 0.0) for c in range(6)], axis=0
    )
    at_depth = (lax.broadcasted_iota(jnp.int32, (128, 128), 0) == (place % 128)).astype(jnp.float32)
    source[...] = lax.dot_general(
        spread,
        at_depth,
        (((1,), (1,)), ((), ())),
        precision=lax.Precision.HIGHEST,
        preferred_element_type=jnp.float32,
    )
    for x in range(8):
        damping = jnp.where(absorb[x] == 1, SPONGE, 1.0)
        weight[0, x] = damping
        put(PUSH, x, 0, "B", H * material[2, x] * damping)
        grown = 1.0 - 0.5 * anelastic[1, x]
        weight[2, x] = grown
        put(PP, x, 0, "B", H * grown * material[0, x])
        put(QQ, x, 0, "B", H * grown * material[1, x])
        cohesion = jnp.zeros((8, 128), jnp.float32)
        friction = jnp.zeros((8, 128), jnp.float32)
        for z in range(ZONES):
            inside = zone[x] == z
            cohesion = jnp.where(inside, cohesion_table[z], cohesion)
            friction = jnp.where(inside, friction_table[z], friction)
        put(COH, x, 0, "B", cohesion)
        put(FRI, x, 0, "B", friction)

    ALL = (CXX, CYY, CZZ, CXY, CXZ, CYZ)
    F_STARTS = (-1, 1)

    for step in range(STEPS):
        kind = step
        for x in range(8):
            keep = 0.5 + 0.5 * anelastic[0, x]
            for c, field in enumerate(ALL):
                base = stress[c, x] + source[pl.ds(c * 64 + x * 8, 8), :] - keep * memory[c, x]
                put(field, x, 0, "B", base)
        for field in (RX, RY, RZ):
            for x in (-2, -1, 8, 9, 10):
                put(field, x, -4, "B", nothing)
                put(field, x, 4, "B", nothing)
        for field, source_field, axis, reach in (
            (RX, SXX, 0, -1),
            (RY, SXY, 0, -2),
            (RZ, SXZ, 0, -2),
            (RY, SYY, 1, -1),
            (RX, SXY, 1, -2),
            (RZ, SYZ, 1, -2),
        ):
            factors = (-FAR, -NEAR, NEAR, FAR)
            for i in (-2, -1, 8, 9, 10):
                total = None
                for k in range(4):
                    j = i + reach + k
                    if 0 <= j < 8:
                        term = factors[k] * (
                            view(source_field, j, 0, "B") if axis == 0 else view(source_field, 0, j, "F")
                        )
                        total = term if total is None else total + term
                if axis == 0:
                    if total is not None:
                        put(field, i, 0, "B", total)
                else:
                    put(field, 0, i, "F", nothing if total is None else total)
        for x in range(8):
            rate_x = (
                forward(SXX, x, 0, "B", 0) + backward(SXY, x, 0, "B", 1) + backward_z(stress[4, x])
            )
            rate_y = (
                backward(SXY, x, 0, "B", 0) + forward(SYY, x, 0, "B", 1) + backward_z(stress[5, x])
            )
            rate_z = (
                backward(SXZ, x, 0, "B", 0) + backward(SYZ, x, 0, "B", 1) + forward_z(stress[2, x])
            )
            damping, push = weight[0, x], view(PUSH, x, 0, "B")
            for c, (field, rate) in enumerate(((VX, rate_x), (VY, rate_y), (VZ, rate_z))):
                before = view(field, x, 0, "B") if step else velocity[c, x]
                put(field, x, 0, "B", before * damping + push * rate)
        pack(kind)
        if step == 0:
            pl.semaphore_wait(barrier, sum(there[d].astype(jnp.int32) for d in SIDES))
        send(kind)
        last = step == STEPS - 1
        receive(kind)
        for field, rates in ((VX, RX), (VY, RY), (VZ, RZ)):
            beside = [(x, y, "B") for x in (-2, -1, 8, 9, 10) for y in (-4, 4)]
            for x, y, form in beside + [(0, y, "F") for y in (-2, -1, 8, 9, 10)]:
                new = view(field, x, y, form) + view(PUSH, x, y, form) * view(rates, x, y, form)
                put(field, x, y, form, new)
        if last:
            for x in range(8):
                for c, field in enumerate((VX, VY, VZ)):
                    velocity[c, x] = view(field, x, 0, "B")

        def shear_xy(x, y, form):
            return forward(VX, x, y, form, 1) + forward(VY, x, y, form, 0)

        def shear_xz(x, y, form):
            return forward_z(view(VX, x, y, form)) + forward(VZ, x, y, form, 0)

        def shear_yz(x, y, form):
            return forward_z(view(VY, x, y, form)) + forward(VZ, x, y, form, 1)

        def normal(x, y, form):
            return (
                backward(VX, x, y, form, 0),
                backward(VY, x, y, form, 1),
                backward_z(view(VZ, x, y, form)),
            )

        def put_shear(field, x, y, form, value):
            put(field, x, y, form, value if field == TXY else value + deeper(value, -1))

        def keep_centre(k, x, y, form, trial):
            mean = (trial[0] + trial[1] + trial[2]) * (1.0 / 3.0)
            dev = [t - mean for t in trial]
            cohesion = view(COH, x, y, form)
            limit = jnp.maximum(cohesion - view(FRI, x, y, form) * mean, 0.25 * cohesion)
            centre[k, 0] = 0.5 * (dev[0] * dev[0] + dev[1] * dev[1] + dev[2] * dev[2])
            centre[k, 1] = limit
            if k < 8:
                centre[k, 2] = mean
                for c in range(3):
                    centre[k, 3 + c] = dev[c]

        for x in range(8):
            parts = normal(x, 0, "B")
            volume = parts[0] + parts[1] + parts[2]
            lame, modulus = H * material[0, x], H * material[1, x]
            spread_out = lame * volume
            rates = [spread_out + 2.0 * modulus * e for e in parts] + [
                modulus * e
                for e in (shear_xy(x, 0, "B"), shear_xz(x, 0, "B"), shear_yz(x, 0, "B"))
            ]
            grown, decay, share = weight[2, x], anelastic[0, x], anelastic[1, x]
            trial = []
            for c, field in enumerate(ALL):
                trial.append(view(field, x, 0, "B") + grown * rates[c])
                memory[c, x] = decay * memory[c, x] + share * rates[c]
            for c, field in ((3, TXY), (4, UXZ), (5, UYZ)):
                put_shear(field, x, 0, "B", trial[c])
                centre[x, 3 + c] = trial[c]
            keep_centre(x, x, 0, "B", trial[:3])
        beyond = [(8, 8, 0, "B")] + [(9 + k, x, 8, "F") for k, x in enumerate(F_STARTS)]
        for k, x, y, form in beyond:
            parts = normal(x, y, form)
            volume = parts[0] + parts[1] + parts[2]
            lame, modulus = view(PP, x, y, form), view(QQ, x, y, form)
            trial = [
                view(field, x, y, form) + lame * volume + 2.0 * modulus * e
                for field, e in zip(ALL, parts)
            ]
            keep_centre(k, x, y, form, trial)
            for field, base, e in (
                (TXY, CXY, shear_xy(x, y, form)),
                (UXZ, CXZ, shear_xz(x, y, form)),
                (UYZ, CYZ, shear_yz(x, y, form)),
            ):
                put_shear(field, x, y, form, view(base, x, y, form) + modulus * e)
        modulus = view(QQ, -1, 0, "B")
        put_shear(TXY, -1, 0, "B", view(CXY, -1, 0, "B") + modulus * shear_xy(-1, 0, "B"))
        put_shear(UXZ, -1, 0, "B", view(CXZ, -1, 0, "B") + modulus * shear_xz(-1, 0, "B"))
        for x in F_STARTS:
            modulus = view(QQ, x, -1, "F")
            put_shear(TXY, x, -1, "F", view(CXY, x, -1, "F") + modulus * shear_xy(x, -1, "F"))
            put_shear(UYZ, x, -1, "F", view(CYZ, x, -1, "F") + modulus * shear_yz(x, -1, "F"))

        for k, x, y, form in [(x, x, 0, "B") for x in range(8)] + beyond:
            mean_xy = 0.25 * (
                (view(TXY, x - 1, y - 1, form) + view(TXY, x - 1, y, form))
                + (view(TXY, x, y - 1, form) + view(TXY, x, y, form))
            )
            mean_xz = 0.25 * (view(UXZ, x - 1, y, form) + view(UXZ, x, y, form))
            mean_yz = 0.25 * (view(UYZ, x, y - 1, form) + view(UYZ, x, y, form))
            tau = jnp.sqrt(
                centre[k, 0] + mean_xy * mean_xy + mean_xz * mean_xz + mean_yz * mean_yz
            )
            ratio = jnp.minimum(1.0, centre[k, 1] / jnp.maximum(tau, 0.5))
            deficit = 1.0 - ratio
            put(DEF, x, y, form, deficit)
            put(DEZ, x, y, form, deficit + deeper(deficit, 1))
            if k < 8:
                centre[k, 1] = ratio

        for x in range(8):
            ratio, mean = centre[x, 1], centre[x, 2]
            new = [mean + ratio * centre[x, 3 + c] for c in range(3)]
            lack = [view(DEF, x + i, j, "B") for i in (0, 1) for j in (0, 1)]
            new.append((1.0 - 0.25 * ((lack[0] + lack[1]) + (lack[2] + lack[3]))) * centre[x, 6])
            here = view(DEZ, x, 0, "B")
            new.append((1.0 - 0.25 * (here + view(DEZ, x + 1, 0, "B"))) * centre[x, 7])
            new.append((1.0 - 0.25 * (here + view(DEZ, x, 1, "B"))) * centre[x, 8])
            for c in range(6):
                stress[c, x] = new[c]
            if not last:
                for field, c in ((SXX, 0), (SXY, 3), (SXZ, 4), (SYY, 1), (SYZ, 5)):
                    put(field, x, 0, "B", new[c])

    for kind, table in enumerate(MESSAGES):
        for d in table:

            @pl.when(there[d])
            def _():
                copy_of(kind, d, d).wait_send()


def hand_over(*refs):
    n = (len(refs) - 1) // 2
    copies = [pltpu.make_async_copy(refs[k], refs[n + k], refs[-1].at[k]) for k in range(n)]
    for copy in copies:
        copy.start()
    for copy in copies:
        copy.wait()


def shards(
    n_gx,
    n_gy,
    velocity,
    stress,
    memory,
    material,
    anelastic,
    zone_ids,
    absorb_mask,
    source_cells,
    source_moment,
    cohesion_table,
    friction_table,
):
    far = pl.BlockSpec(memory_space=pl.ANY)
    near = pl.BlockSpec(memory_space=pltpu.VMEM)
    f32, i32 = jnp.float32, jnp.int32
    block = (8, 8, 128)
    operands = (
        velocity,
        stress,
        memory,
        material,
        anelastic,
        zone_ids,
        absorb_mask,
        source_cells,
        jnp.swapaxes(source_moment, 1, 2),
        cohesion_table,
        friction_table,
    )
    results = pl.pallas_call(
        functools.partial(kernel, n_gx, n_gy),
        out_shape=[pltpu.VMEM((n, *block), f32) for n in (3, 6, 6)],
        in_specs=[far] * 11,
        out_specs=[near] * 3,
        scratch_shapes=[
            pltpu.VMEM((FIELDS, SLABS * PITCH, 128), f32),
            pltpu.VMEM((BUFFER_ROWS, 128), f32),
            pltpu.VMEM((BUFFER_ROWS, 128), f32),
            pltpu.VMEM((3, *block), f32),
            pltpu.VMEM((2, *block), f32),
            pltpu.VMEM(block, i32),
            pltpu.VMEM(block, i32),
            pltpu.VMEM((1, 1, 128), i32),
            pltpu.VMEM((1, 6, 1, 128), f32),
            pltpu.SMEM((ZONES,), f32),
            pltpu.SMEM((ZONES,), f32),
            pltpu.VMEM((6 * 64, 128), f32),
            pltpu.VMEM((3, *block), f32),
            pltpu.VMEM((11, 9, 8, 128), f32),
            pltpu.SemaphoreType.DMA((N_MESSAGES,)),
            pltpu.SemaphoreType.DMA((N_MESSAGES,)),
            pltpu.SemaphoreType.DMA((11,)),
        ],
        compiler_params=pltpu.CompilerParams(
            collective_id=0, has_side_effects=True, vmem_limit_bytes=32 * 2**20
        ),
        name="waves",
    )(*[pltpu.with_memory_space_constraint(x, pltpu.HBM) for x in operands])
    return tuple(
        pl.pallas_call(
            hand_over,
            out_shape=[jax.ShapeDtypeStruct(r.shape, r.dtype) for r in results],
            in_specs=[near] * 3,
            out_specs=[far] * 3,
            scratch_shapes=[pltpu.SemaphoreType.DMA((3,))],
            name="results",
        )(*[pltpu.with_memory_space_constraint(r, pltpu.VMEM) for r in results])
    )


def solution(mesh):
    in_specs = (
        P(None, "gx", "gy", None),
        P(None, "gx", "gy", None),
        P(None, "gx", "gy", None),
        P(None, "gx", "gy", None),
        P(None, "gx", "gy", None),
        P("gx", "gy", None),
        P("gx", "gy", None),
        P("gx", "gy", None),
        P("gx", "gy", None, None),
        P(),
        P(),
    )
    out_specs = (P(None, "gx", "gy", None), P(None, "gx", "gy", None), P(None, "gx", "gy", None))
    body = functools.partial(shards, mesh.shape["gx"], mesh.shape["gy"])
    return jax.shard_map(body, mesh=mesh, in_specs=in_specs, out_specs=out_specs, check_vma=False)
```

```python
import functools

import jax
import jax.numpy as jnp
from jax import lax
from jax.experimental import pallas as pl
from jax.experimental.pallas import tpu as pltpu
from jax.sharding import PartitionSpec as P

MESH = pl.DeviceIdType.MESH
STEPS = 2
ZONES = 8
NEAR = 9.0 / 8.0
FAR = -1.0 / 24.0
H = 0.12
SPONGE = 0.92
OPEN = 1.0e9

SXX, SXY, SXZ, SYY, SYZ, VX, VY, VZ, RX, RY, RZ = range(11)
CXX, CYY, CZZ, CXY, CXZ, CYZ = range(11, 17)
PP, QQ, COH, FRI, PUSH = range(17, 22)
TXY, UXZ, UYZ, DEF, DEZ = range(22, 27)
FIELDS = 27
SLABS = 14
PITCH = 16

FACES = ((-1, 0), (1, 0), (0, -1), (0, 1))
CORNERS = ((-1, -1), (-1, 1), (1, -1), (1, 1))
SIDES = FACES + CORNERS


def row(x, y):
    return (x + 3) * PITCH + (y + 4)


def xs(field, x):
    return (field, "B", x, 0, 8)


def ys(field, y):
    return (field, "F", 0, y, 8)


def some(field, x, y, n=1):
    return (field, "B", x, y, n)


def boxes(*parts):
    return [some(f, x, y, n) for f, x, y, n in parts]


def rows_x(field, *at):
    return [xs(field, x) for x in at]


def rows_y(field, *at):
    return [ys(field, y) for y in at]


NORMAL_AND_SHEAR = (CXX, CYY, CZZ, CXY, CXZ, CYZ)

EACH_STEP = {
    (1, 0): rows_x(VX, 6, 7) + rows_x(VY, 6, 7) + rows_x(VZ, 6, 7)
    + rows_x(RX, 8) + rows_x(RY, 8, 9) + rows_x(RZ, 8, 9) + rows_x(CXY, 7) + rows_x(CXZ, 7)
    + boxes((RX, 7, 8, 2), (RX, 6, 8, 1), (RY, 6, 8, 1), (RY, 7, 8, 1), (RZ, 6, 8, 1), (RZ, 7, 8, 1))
    + boxes((RX, 7, -1, 1), (RY, 6, -1, 1), (RY, 7, -1, 1)),
    (-1, 0): rows_x(VX, 0, 1) + rows_x(VY, 0, 1, 2) + rows_x(VZ, 0, 1, 2)
    + rows_x(RX, -2, -1) + rows_x(RY, -1) + rows_x(RZ, -1)
    + [xs(f, 0) for f in NORMAL_AND_SHEAR]
    + boxes((RX, 0, 8, 2), (RX, 1, 8, 1), (RY, 0, 8, 1), (RY, 1, 8, 1), (RY, 2, 8, 1))
    + boxes((RZ, 0, 8, 2), (RZ, 1, 8, 1), (RZ, 2, 8, 1))
    + boxes((RX, 0, -1, 1), (RY, 0, -2, 2), (RY, 1, -1, 1), (RY, 2, -1, 1), (RZ, 0, -1, 1)),
    (0, 1): rows_y(VX, 6, 7) + rows_y(VY, 6, 7) + rows_y(VZ, 6, 7)
    + rows_y(RY, 8) + rows_y(RX, 8, 9) + rows_y(RZ, 8, 9) + rows_y(CXY, 7) + rows_y(CYZ, 7)
    + boxes((RX, 8, 6, 2), (RY, 8, 6, 2), (RY, 9, 7, 1), (RZ, 8, 6, 2))
    + boxes((RX, -1, 6, 2), (RY, -1, 7, 1)),
    (0, -1): rows_y(VY, 0, 1) + rows_y(VX, 0, 1, 2) + rows_y(VZ, 0, 1, 2)
    + rows_y(RY, -2, -1) + rows_y(RX, -1) + rows_y(RZ, -1)
    + [ys(f, 0) for f in NORMAL_AND_SHEAR]
    + boxes((RX, 8, 0, 3), (RY, 8, 0, 2), (RY, 9, 0, 1), (RZ, 8, 0, 3), (RZ, 9, 0, 1))
    + boxes((RX, -1, 0, 3), (RX, -2, 0, 1), (RY, -1, 0, 1), (RZ, -1, 0, 1)),
    (1, 1): boxes((VX, 7, 6, 2), (VY, 6, 7, 1), (VY, 7, 7, 1), (CXY, 7, 7, 1))
    + boxes((RX, 6, 8, 2), (RX, 7, 8, 2), (RY, 6, 8, 1), (RY, 7, 8, 1), (RZ, 6, 8, 2), (RZ, 7, 8, 2))
    + boxes((RX, 8, 6, 2), (RY, 8, 6, 2), (RY, 9, 6, 2), (RZ, 8, 6, 2), (RZ, 9, 6, 2)),
    (-1, -1): boxes((VX, 0, 0, 3), (VX, 1, 0, 1), (VY, 0, 0, 2), (VY, 1, 0, 1), (VY, 2, 0, 1))
    + boxes((VZ, 0, 0, 3), (VZ, 1, 0, 1), (VZ, 2, 0, 1))
    + [some(f, 0, 0) for f in NORMAL_AND_SHEAR]
    + boxes((RX, 0, -1, 1), (RX, 1, -1, 1), (RY, 0, -2, 2), (RY, 1, -2, 2), (RY, 2, -2, 2))
    + boxes((RZ, 0, -1, 1), (RZ, 1, -1, 1), (RZ, 2, -1, 1))
    + boxes((RX, -2, 0, 3), (RX, -1, 0, 3), (RY, -1, 0, 2), (RZ, -1, 0, 3)),
    (-1, 1): boxes((VX, 0, 6, 2), (VY, 0, 6, 2), (VY, 1, 7, 1), (VY, 2, 7, 1), (VZ, 0, 6, 2))
    + boxes((CXY, 0, 7, 1), (CYZ, 0, 7, 1))
    + boxes((RX, 0, 8, 2), (RX, 1, 8, 2), (RY, 0, 8, 1), (RY, 1, 8, 1), (RY, 2, 8, 1))
    + boxes((RZ, 0, 8, 2), (RZ, 1, 8, 2), (RZ, 2, 8, 2))
    + boxes((RX, -2, 6, 2), (RX, -1, 6, 2), (RY, -1, 6, 2), (RZ, -1, 6, 2)),
    (1, -1): boxes((VX, 7, 0, 3), (VX, 6, 0, 1), (VY, 6, 0, 1), (VY, 7, 0, 1), (VZ, 6, 0, 1), (VZ, 7, 0, 1))
    + boxes((CXY, 7, 0, 1), (CXZ, 7, 0, 1))
    + boxes((RX, 6, -1, 1), (RX, 7, -1, 1), (RY, 6, -2, 2), (RY, 7, -2, 2), (RZ, 6, -1, 1), (RZ, 7, -1, 1))
    + boxes((RX, 8, 0, 3), (RY, 8, 0, 2), (RY, 9, 0, 2), (RZ, 8, 0, 3), (RZ, 9, 0, 3)),
}
ONCE = {
    (1, 0): rows_x(QQ, 7) + rows_x(PUSH, 6, 7),
    (-1, 0): [xs(f, 0) for f in (PP, QQ, COH, FRI)] + rows_x(PUSH, 0, 1, 2),
    (0, 1): rows_y(QQ, 7) + rows_y(PUSH, 6, 7),
    (0, -1): [ys(f, 0) for f in (PP, QQ, COH, FRI)] + rows_y(PUSH, 0, 1, 2),
    (1, 1): boxes((QQ, 7, 7, 1), (PUSH, 7, 6, 2), (PUSH, 6, 7, 1)),
    (-1, -1): [some(f, 0, 0) for f in (PP, QQ, COH, FRI)]
    + boxes((PUSH, 0, 0, 3), (PUSH, 1, 0, 1), (PUSH, 2, 0, 1)),
    (-1, 1): boxes((QQ, 0, 7, 1), (PUSH, 0, 6, 2), (PUSH, 1, 7, 1), (PUSH, 2, 7, 1)),
    (1, -1): boxes((QQ, 7, 0, 1), (PUSH, 7, 0, 3), (PUSH, 6, 0, 1)),
}


def rows_of(items):
    return -(-sum(item[4] for item in items) // 8) * 8


MESSAGES = [{d: ONCE[d] + EACH_STEP[d] for d in SIDES}, EACH_STEP]

PLACES = {}
used = 0
for kind, table in enumerate(MESSAGES):
    for side, sent in table.items():
        PLACES[kind, side] = (used, rows_of(sent), len(PLACES))
        used += rows_of(sent)
BUFFER_ROWS = used
N_MESSAGES = len(PLACES)


def kernel(
    n_gx,
    n_gy,
    velocity_in,
    stress_in,
    memory_in,
    material_in,
    anelastic_in,
    zone_in,
    absorb_in,
    cells_in,
    moment_in,
    cohesion_in,
    friction_in,
    velocity,
    stress,
    memory,
    ext,
    sent,
    received,
    material,
    anelastic,
    zone,
    absorb,
    cells,
    moment,
    cohesion_table,
    friction_table,
    source,
    weight,
    centre,
    send_sem,
    recv_sem,
    in_sem,
):
    gx, gy = lax.axis_index("gx"), lax.axis_index("gy")
    there = {}
    for dx, dy in SIDES:
        checks = []
        if dx:
            checks.append(gx > 0 if dx < 0 else gx < n_gx - 1)
        if dy:
            checks.append(gy > 0 if dy < 0 else gy < n_gy - 1)
        there[dx, dy] = checks[0] if len(checks) == 1 else jnp.logical_and(*checks)

    def device(d):
        return (gx + d[0], gy + d[1])

    barrier = pltpu.get_barrier_semaphore()
    for d in SIDES:

        @pl.when(there[d])
        def _():
            pl.semaphore_signal(barrier, 1, device_id=device(d), device_id_type=MESH)

    loads = []
    for k, (src, dst) in enumerate(
        (
            (stress_in, stress),
            (velocity_in, velocity),
            (memory_in, memory),
            (material_in, material),
            (anelastic_in, anelastic),
            (zone_in, zone),
            (absorb_in, absorb),
            (cells_in, cells),
            (moment_in, moment),
            (cohesion_in, cohesion_table),
            (friction_in, friction_table),
        )
    ):
        loads.append(pltpu.make_async_copy(src, dst, in_sem.at[k]))
        loads[-1].start()

    def spot(field, form, x, y, n):
        start = row(x, y)
        return ext.at[field, pl.ds(start, n) if form == "B" else pl.ds(start, n, stride=PITCH), :]

    def at(item):
        return spot(*item)

    def landed(item, d):
        field, form, x, y, n = item
        return (field, form, x - 8 * d[0], y - 8 * d[1], n)

    def copy_of(kind, d, sem_side):
        start, n, k = PLACES[kind, d]
        n = sum(item[4] for item in MESSAGES[kind][d])
        return pltpu.make_async_remote_copy(
            src_ref=sent.at[pl.ds(start, n)],
            dst_ref=received.at[pl.ds(start, n)],
            send_sem=send_sem.at[k],
            recv_sem=recv_sem.at[k],
            device_id=device(sem_side),
            device_id_type=MESH,
        )

    def pack(kind):
        for d, items in MESSAGES[kind].items():
            start = PLACES[kind, d][0]
            for item in items:
                sent[pl.ds(start, item[4]), :] = at(item)[...]
                start += item[4]

    def send(kind):
        for d in CORNERS + FACES:

            @pl.when(there[d])
            def _():
                copy_of(kind, d, d).start()

    def receive(kind):
        for d, items in MESSAGES[kind].items():
            back = (-d[0], -d[1])

            @pl.when(there[back])
            def _():
                copy_of(kind, d, back).wait_recv()
                start = PLACES[kind, d][0]
                for item in items:
                    value = received[pl.ds(start, item[4]), :]
                    start += item[4]
                    field, form, x, y, n = landed(item, d)
                    if field in (RX, RY, RZ) and 0 <= x < 8 and 0 <= y < 8:
                        mine = spot(field - RX + VX, form, x, y, n)
                        mine[...] = mine[...] + spot(PUSH, form, x, y, n)[...] * value
                    elif field in (RX, RY, RZ):
                        rates = spot(field, form, x, y, n)
                        rates[...] = rates[...] + value
                    else:
                        spot(field, form, x, y, n)[...] = value

    def outside(kind):
        for d, items in MESSAGES[kind].items():

            @pl.when(jnp.logical_not(there[-d[0], -d[1]]))
            def _():
                for item in items:
                    if item[0] not in (RX, RY, RZ):
                        value = OPEN if item[0] == COH else 0.0
                        spot(*landed(item, d))[...] = jnp.full((item[4], 128), value, jnp.float32)

    depth = lax.broadcasted_iota(jnp.int32, (8, 128), 1)

    def deeper(f, n):
        moved = pltpu.roll(f, (-n) % 128, 1)
        return jnp.where((depth < 128 - n) if n > 0 else (depth >= -n), moved, 0.0)

    def view(field, x, y, form):
        start = row(x, y)
        return ext[field, pl.ds(start, 8) if form == "B" else pl.ds(start, 8, stride=PITCH), :]

    def put(field, x, y, form, value):
        start = row(x, y)
        ext[field, pl.ds(start, 8) if form == "B" else pl.ds(start, 8, stride=PITCH), :] = value

    def along(field, x, y, form, axis, first):
        f = [
            view(field, x + (first + k if axis == 0 else 0), y + (first + k if axis == 1 else 0), form)
            for k in range(4)
        ]
        return NEAR * (f[2] - f[1]) + FAR * (f[3] - f[0])

    def forward(field, x, y, form, axis):
        return along(field, x, y, form, axis, -1)

    def backward(field, x, y, form, axis):
        return along(field, x, y, form, axis, -2)

    def forward_z(f):
        return NEAR * (deeper(f, 1) - f) + FAR * (deeper(f, 2) - deeper(f, -1))

    def backward_z(f):
        return NEAR * (f - deeper(f, -1)) + FAR * (deeper(f, 1) - deeper(f, -2))

    nothing = jnp.zeros((8, 128), jnp.float32)
    for field in (SXX, SXY, SXZ, SYY, SYZ):
        for x in (-2, -1, 8, 9):
            put(field, x, -4, "B", nothing)
            put(field, x, 4, "B", nothing)
        for y in (-2, -1, 8, 9):
            put(field, 0, y, "F", nothing)
    outside(0)
    loads[0].wait()
    for x in range(8):
        for field, c in ((SXX, 0), (SXY, 3), (SXZ, 4), (SYY, 1), (SYZ, 5)):
            put(field, x, 0, "B", stress[c, x])

    for k, load in enumerate(loads):
        if k:
            load.wait()
    place = cells[0]
    column = lax.broadcasted_iota(jnp.int32, (64, 128), 0) == (place // 128)
    spread = jnp.concatenate(
        [jnp.where(column, H * moment[0, c], 0.0) for c in range(6)], axis=0
    )
    at_depth = (lax.broadcasted_iota(jnp.int32, (128, 128), 0) == (place % 128)).astype(jnp.float32)
    source[...] = lax.dot_general(
        spread,
        at_depth,
        (((1,), (1,)), ((), ())),
        precision=lax.Precision.HIGHEST,
        preferred_element_type=jnp.float32,
    )
    for x in range(8):
        damping = jnp.where(absorb[x] == 1, SPONGE, 1.0)
        weight[0, x] = damping
        put(PUSH, x, 0, "B", H * material[2, x] * damping)
        grown = 1.0 - 0.5 * anelastic[1, x]
        weight[2, x] = grown
        put(PP, x, 0, "B", H * grown * material[0, x])
        put(QQ, x, 0, "B", H * grown * material[1, x])
        cohesion = jnp.zeros((8, 128), jnp.float32)
        friction = jnp.zeros((8, 128), jnp.float32)
        for z in range(ZONES):
            inside = zone[x] == z
            cohesion = jnp.where(inside, cohesion_table[z], cohesion)
            friction = jnp.where(inside, friction_table[z], friction)
        put(COH, x, 0, "B", cohesion)
        put(FRI, x, 0, "B", friction)

    ALL = (CXX, CYY, CZZ, CXY, CXZ, CYZ)
    F_STARTS = (-1, 1)

    for step in range(STEPS):
        kind = step
        for x in range(8):
            keep = 0.5 + 0.5 * anelastic[0, x]
            for c, field in enumerate(ALL):
                base = stress[c, x] + source[pl.ds(c * 64 + x * 8, 8), :] - keep * memory[c, x]
                put(field, x, 0, "B", base)
        for field in (RX, RY, RZ):
            for x in (-2, -1, 8, 9, 10):
                put(field, x, -4, "B", nothing)
                put(field, x, 4, "B", nothing)
        for field, source_field, axis, reach in (
            (RX, SXX, 0, -1),
            (RY, SXY, 0, -2),
            (RZ, SXZ, 0, -2),
            (RY, SYY, 1, -1),
            (RX, SXY, 1, -2),
            (RZ, SYZ, 1, -2),
        ):
            factors = (-FAR, -NEAR, NEAR, FAR)
            for i in (-2, -1, 8, 9, 10):
                total = None
                for k in range(4):
                    j = i + reach + k
                    if 0 <= j < 8:
                        term = factors[k] * (
                            view(source_field, j, 0, "B") if axis == 0 else view(source_field, 0, j, "F")
                        )
                        total = term if total is None else total + term
                if axis == 0:
                    if total is not None:
                        put(field, i, 0, "B", total)
                else:
                    put(field, 0, i, "F", nothing if total is None else total)
        for x in range(8):
            rate_x = (
                forward(SXX, x, 0, "B", 0) + backward(SXY, x, 0, "B", 1) + backward_z(stress[4, x])
            )
            rate_y = (
                backward(SXY, x, 0, "B", 0) + forward(SYY, x, 0, "B", 1) + backward_z(stress[5, x])
            )
            rate_z = (
                backward(SXZ, x, 0, "B", 0) + backward(SYZ, x, 0, "B", 1) + forward_z(stress[2, x])
            )
            damping, push = weight[0, x], view(PUSH, x, 0, "B")
            for c, (field, rate) in enumerate(((VX, rate_x), (VY, rate_y), (VZ, rate_z))):
                before = view(field, x, 0, "B") if step else velocity[c, x]
                put(field, x, 0, "B", before * damping + push * rate)
        pack(kind)
        if step == 0:
            pl.semaphore_wait(barrier, sum(there[d].astype(jnp.int32) for d in SIDES))
        send(kind)
        last = step == STEPS - 1
        receive(kind)
        for field, rates in ((VX, RX), (VY, RY), (VZ, RZ)):
            beside = [(x, y, "B") for x in (-2, -1, 8, 9, 10) for y in (-4, 4)]
            for x, y, form in beside + [(0, y, "F") for y in (-2, -1, 8, 9, 10)]:
                new = view(field, x, y, form) + view(PUSH, x, y, form) * view(rates, x, y, form)
                put(field, x, y, form, new)
        if last:
            for x in range(8):
                for c, field in enumerate((VX, VY, VZ)):
                    velocity[c, x] = view(field, x, 0, "B")

        def shear_xy(x, y, form):
            return forward(VX, x, y, form, 1) + forward(VY, x, y, form, 0)

        def shear_xz(x, y, form):
            return forward_z(view(VX, x, y, form)) + forward(VZ, x, y, form, 0)

        def shear_yz(x, y, form):
            return forward_z(view(VY, x, y, form)) + forward(VZ, x, y, form, 1)

        def normal(x, y, form):
            return (
                backward(VX, x, y, form, 0),
                backward(VY, x, y, form, 1),
                backward_z(view(VZ, x, y, form)),
            )

        def put_shear(field, x, y, form, value):
            put(field, x, y, form, value if field == TXY else value + deeper(value, -1))

        def keep_centre(k, x, y, form, trial):
            mean = (trial[0] + trial[1] + trial[2]) * (1.0 / 3.0)
            dev = [t - mean for t in trial]
            cohesion = view(COH, x, y, form)
            limit = jnp.maximum(cohesion - view(FRI, x, y, form) * mean, 0.25 * cohesion)
            centre[k, 0] = 0.5 * (dev[0] * dev[0] + dev[1] * dev[1] + dev[2] * dev[2])
            centre[k, 1] = limit
            if k < 8:
                centre[k, 2] = mean
                for c in range(3):
                    centre[k, 3 + c] = dev[c]

        for x in range(8):
            parts = normal(x, 0, "B")
            volume = parts[0] + parts[1] + parts[2]
            lame, modulus = H * material[0, x], H * material[1, x]
            spread_out = lame * volume
            rates = [spread_out + 2.0 * modulus * e for e in parts] + [
                modulus * e
                for e in (shear_xy(x, 0, "B"), shear_xz(x, 0, "B"), shear_yz(x, 0, "B"))
            ]
            grown, decay, share = weight[2, x], anelastic[0, x], anelastic[1, x]
            trial = []
            for c, field in enumerate(ALL):
                trial.append(view(field, x, 0, "B") + grown * rates[c])
                memory[c, x] = decay * memory[c, x] + share * rates[c]
            for c, field in ((3, TXY), (4, UXZ), (5, UYZ)):
                put_shear(field, x, 0, "B", trial[c])
                centre[x, 3 + c] = trial[c]
            keep_centre(x, x, 0, "B", trial[:3])
        beyond = [(8, 8, 0, "B")] + [(9 + k, x, 8, "F") for k, x in enumerate(F_STARTS)]
        for k, x, y, form in beyond:
            parts = normal(x, y, form)
            volume = parts[0] + parts[1] + parts[2]
            lame, modulus = view(PP, x, y, form), view(QQ, x, y, form)
            trial = [
                view(field, x, y, form) + lame * volume + 2.0 * modulus * e
                for field, e in zip(ALL, parts)
            ]
            keep_centre(k, x, y, form, trial)
            for field, base, e in (
                (TXY, CXY, shear_xy(x, y, form)),
                (UXZ, CXZ, shear_xz(x, y, form)),
                (UYZ, CYZ, shear_yz(x, y, form)),
            ):
                put_shear(field, x, y, form, view(base, x, y, form) + modulus * e)
        modulus = view(QQ, -1, 0, "B")
        put_shear(TXY, -1, 0, "B", view(CXY, -1, 0, "B") + modulus * shear_xy(-1, 0, "B"))
        put_shear(UXZ, -1, 0, "B", view(CXZ, -1, 0, "B") + modulus * shear_xz(-1, 0, "B"))
        for x in F_STARTS:
            modulus = view(QQ, x, -1, "F")
            put_shear(TXY, x, -1, "F", view(CXY, x, -1, "F") + modulus * shear_xy(x, -1, "F"))
            put_shear(UYZ, x, -1, "F", view(CYZ, x, -1, "F") + modulus * shear_yz(x, -1, "F"))

        for k, x, y, form in [(x, x, 0, "B") for x in range(8)] + beyond:
            mean_xy = 0.25 * (
                (view(TXY, x - 1, y - 1, form) + view(TXY, x - 1, y, form))
                + (view(TXY, x, y - 1, form) + view(TXY, x, y, form))
            )
            mean_xz = 0.25 * (view(UXZ, x - 1, y, form) + view(UXZ, x, y, form))
            mean_yz = 0.25 * (view(UYZ, x, y - 1, form) + view(UYZ, x, y, form))
            tau = jnp.sqrt(
                centre[k, 0] + mean_xy * mean_xy + mean_xz * mean_xz + mean_yz * mean_yz
            )
            ratio = jnp.minimum(1.0, centre[k, 1] / jnp.maximum(tau, 0.5))
            deficit = 1.0 - ratio
            put(DEF, x, y, form, deficit)
            put(DEZ, x, y, form, deficit + deeper(deficit, 1))
            if k < 8:
                centre[k, 1] = ratio

        for x in range(8):
            ratio, mean = centre[x, 1], centre[x, 2]
            new = [mean + ratio * centre[x, 3 + c] for c in range(3)]
            lack = [view(DEF, x + i, j, "B") for i in (0, 1) for j in (0, 1)]
            new.append((1.0 - 0.25 * ((lack[0] + lack[1]) + (lack[2] + lack[3]))) * centre[x, 6])
            here = view(DEZ, x, 0, "B")
            new.append((1.0 - 0.25 * (here + view(DEZ, x + 1, 0, "B"))) * centre[x, 7])
            new.append((1.0 - 0.25 * (here + view(DEZ, x, 1, "B"))) * centre[x, 8])
            for c in range(6):
                stress[c, x] = new[c]
            if not last:
                for field, c in ((SXX, 0), (SXY, 3), (SXZ, 4), (SYY, 1), (SYZ, 5)):
                    put(field, x, 0, "B", new[c])

    for kind, table in enumerate(MESSAGES):
        for d in table:

            @pl.when(there[d])
            def _():
                copy_of(kind, d, d).wait_send()


def hand_over(*refs):
    n = (len(refs) - 1) // 2
    copies = [pltpu.make_async_copy(refs[k], refs[n + k], refs[-1].at[k]) for k in range(n)]
    for copy in copies:
        copy.start()
    for copy in copies:
        copy.wait()


def shards(
    n_gx,
    n_gy,
    velocity,
    stress,
    memory,
    material,
    anelastic,
    zone_ids,
    absorb_mask,
    source_cells,
    source_moment,
    cohesion_table,
    friction_table,
):
    far = pl.BlockSpec(memory_space=pl.ANY)
    near = pl.BlockSpec(memory_space=pltpu.VMEM)
    f32, i32 = jnp.float32, jnp.int32
    block = (8, 8, 128)
    operands = (
        velocity,
        stress,
        memory,
        material,
        anelastic,
        zone_ids,
        absorb_mask,
        source_cells,
        jnp.swapaxes(source_moment, 1, 2),
        cohesion_table,
        friction_table,
    )
    results = pl.pallas_call(
        functools.partial(kernel, n_gx, n_gy),
        out_shape=[pltpu.VMEM((n, *block), f32) for n in (3, 6, 6)],
        in_specs=[far] * 11,
        out_specs=[near] * 3,
        scratch_shapes=[
            pltpu.VMEM((FIELDS, SLABS * PITCH, 128), f32),
            pltpu.VMEM((BUFFER_ROWS, 128), f32),
            pltpu.VMEM((BUFFER_ROWS, 128), f32),
            pltpu.VMEM((3, *block), f32),
            pltpu.VMEM((2, *block), f32),
            pltpu.VMEM(block, i32),
            pltpu.VMEM(block, i32),
            pltpu.VMEM((1, 1, 128), i32),
            pltpu.VMEM((1, 6, 1, 128), f32),
            pltpu.SMEM((ZONES,), f32),
            pltpu.SMEM((ZONES,), f32),
            pltpu.VMEM((6 * 64, 128), f32),
            pltpu.VMEM((3, *block), f32),
            pltpu.VMEM((11, 9, 8, 128), f32),
            pltpu.SemaphoreType.DMA((N_MESSAGES,)),
            pltpu.SemaphoreType.DMA((N_MESSAGES,)),
            pltpu.SemaphoreType.DMA((11,)),
        ],
        compiler_params=pltpu.CompilerParams(
            collective_id=0, has_side_effects=True, vmem_limit_bytes=32 * 2**20
        ),
        name="waves",
    )(*[pltpu.with_memory_space_constraint(x, pltpu.HBM) for x in operands])
    return tuple(
        pl.pallas_call(
            hand_over,
            out_shape=[jax.ShapeDtypeStruct(r.shape, r.dtype) for r in results],
            in_specs=[near] * 3,
            out_specs=[far] * 3,
            scratch_shapes=[pltpu.SemaphoreType.DMA((3,))],
            name="results",
        )(*[pltpu.with_memory_space_constraint(r, pltpu.VMEM) for r in results])
    )


def solution(mesh):
    in_specs = (
        P(None, "gx", "gy", None),
        P(None, "gx", "gy", None),
        P(None, "gx", "gy", None),
        P(None, "gx", "gy", None),
        P(None, "gx", "gy", None),
        P("gx", "gy", None),
        P("gx", "gy", None),
        P("gx", "gy", None),
        P("gx", "gy", None, None),
        P(),
        P(),
    )
    out_specs = (P(None, "gx", "gy", None), P(None, "gx", "gy", None), P(None, "gx", "gy", None))
    body = functools.partial(shards, mesh.shape["gx"], mesh.shape["gy"])
    return jax.shard_map(body, mesh=mesh, in_specs=in_specs, out_specs=out_specs, check_vma=False)
```

```python
import functools

import jax
import jax.numpy as jnp
from jax import lax
from jax.experimental import pallas as pl
from jax.experimental.pallas import tpu as pltpu
from jax.sharding import PartitionSpec as P

MESH = pl.DeviceIdType.MESH
STEPS = 2
ZONES = 8
NEAR = 9.0 / 8.0
FAR = -1.0 / 24.0
H = 0.12
SPONGE = 0.92
OPEN = 1.0e9

SXX, SXY, SXZ, SYY, SYZ, VX, VY, VZ, RX, RY, RZ = range(11)
CXX, CYY, CZZ, CXY, CXZ, CYZ = range(11, 17)
PP, QQ, COH, FRI, PUSH = range(17, 22)
TXY, UXZ, UYZ, DEF, DEZ = range(22, 27)
FIELDS = 27
SLABS = 14
PITCH = 16

FACES = ((-1, 0), (1, 0), (0, -1), (0, 1))
CORNERS = ((-1, -1), (-1, 1), (1, -1), (1, 1))
SIDES = FACES + CORNERS


def row(x, y):
    return (x + 3) * PITCH + (y + 4)


def xs(field, x):
    return (field, "B", x, 0, 8)


def ys(field, y):
    return (field, "F", 0, y, 8)


def some(field, x, y, n=1):
    return (field, "B", x, y, n)


def boxes(*parts):
    return [some(f, x, y, n) for f, x, y, n in parts]


def rows_x(field, *at):
    return [xs(field, x) for x in at]


def rows_y(field, *at):
    return [ys(field, y) for y in at]


NORMAL_AND_SHEAR = (CXX, CYY, CZZ, CXY, CXZ, CYZ)

EACH_STEP = {
    (1, 0): rows_x(VX, 6, 7) + rows_x(VY, 6, 7) + rows_x(VZ, 6, 7)
    + rows_x(RX, 8) + rows_x(RY, 8, 9) + rows_x(RZ, 8, 9) + rows_x(CXY, 7) + rows_x(CXZ, 7)
    + boxes((RX, 7, 8, 2), (RX, 6, 8, 1), (RY, 6, 8, 1), (RY, 7, 8, 1), (RZ, 6, 8, 1), (RZ, 7, 8, 1))
    + boxes((RX, 7, -1, 1), (RY, 6, -1, 1), (RY, 7, -1, 1)),
    (-1, 0): rows_x(VX, 0, 1) + rows_x(VY, 0, 1, 2) + rows_x(VZ, 0, 1, 2)
    + rows_x(RX, -2, -1) + rows_x(RY, -1) + rows_x(RZ, -1)
    + [xs(f, 0) for f in NORMAL_AND_SHEAR]
    + boxes((RX, 0, 8, 2), (RX, 1, 8, 1), (RY, 0, 8, 1), (RY, 1, 8, 1), (RY, 2, 8, 1))
    + boxes((RZ, 0, 8, 2), (RZ, 1, 8, 1), (RZ, 2, 8, 1))
    + boxes((RX, 0, -1, 1), (RY, 0, -2, 2), (RY, 1, -1, 1), (RY, 2, -1, 1), (RZ, 0, -1, 1)),
    (0, 1): rows_y(VX, 6, 7) + rows_y(VY, 6, 7) + rows_y(VZ, 6, 7)
    + rows_y(RY, 8) + rows_y(RX, 8, 9) + rows_y(RZ, 8, 9) + rows_y(CXY, 7) + rows_y(CYZ, 7)
    + boxes((RX, 8, 6, 2), (RY, 8, 6, 2), (RY, 9, 7, 1), (RZ, 8, 6, 2))
    + boxes((RX, -1, 6, 2), (RY, -1, 7, 1)),
    (0, -1): rows_y(VY, 0, 1) + rows_y(VX, 0, 1, 2) + rows_y(VZ, 0, 1, 2)
    + rows_y(RY, -2, -1) + rows_y(RX, -1) + rows_y(RZ, -1)
    + [ys(f, 0) for f in NORMAL_AND_SHEAR]
    + boxes((RX, 8, 0, 3), (RY, 8, 0, 2), (RY, 9, 0, 1), (RZ, 8, 0, 3), (RZ, 9, 0, 1))
    + boxes((RX, -1, 0, 3), (RX, -2, 0, 1), (RY, -1, 0, 1), (RZ, -1, 0, 1)),
    (1, 1): boxes((VX, 7, 6, 2), (VY, 6, 7, 1), (VY, 7, 7, 1), (CXY, 7, 7, 1))
    + boxes((RX, 6, 8, 2), (RX, 7, 8, 2), (RY, 6, 8, 1), (RY, 7, 8, 1), (RZ, 6, 8, 2), (RZ, 7, 8, 2))
    + boxes((RX, 8, 6, 2), (RY, 8, 6, 2), (RY, 9, 6, 2), (RZ, 8, 6, 2), (RZ, 9, 6, 2)),
    (-1, -1): boxes((VX, 0, 0, 3), (VX, 1, 0, 1), (VY, 0, 0, 2), (VY, 1, 0, 1), (VY, 2, 0, 1))
    + boxes((VZ, 0, 0, 3), (VZ, 1, 0, 1), (VZ, 2, 0, 1))
    + [some(f, 0, 0) for f in NORMAL_AND_SHEAR]
    + boxes((RX, 0, -1, 1), (RX, 1, -1, 1), (RY, 0, -2, 2), (RY, 1, -2, 2), (RY, 2, -2, 2))
    + boxes((RZ, 0, -1, 1), (RZ, 1, -1, 1), (RZ, 2, -1, 1))
    + boxes((RX, -2, 0, 3), (RX, -1, 0, 3), (RY, -1, 0, 2), (RZ, -1, 0, 3)),
    (-1, 1): boxes((VX, 0, 6, 2), (VY, 0, 6, 2), (VY, 1, 7, 1), (VY, 2, 7, 1), (VZ, 0, 6, 2))
    + boxes((CXY, 0, 7, 1), (CYZ, 0, 7, 1))
    + boxes((RX, 0, 8, 2), (RX, 1, 8, 2), (RY, 0, 8, 1), (RY, 1, 8, 1), (RY, 2, 8, 1))
    + boxes((RZ, 0, 8, 2), (RZ, 1, 8, 2), (RZ, 2, 8, 2))
    + boxes((RX, -2, 6, 2), (RX, -1, 6, 2), (RY, -1, 6, 2), (RZ, -1, 6, 2)),
    (1, -1): boxes((VX, 7, 0, 3), (VX, 6, 0, 1), (VY, 6, 0, 1), (VY, 7, 0, 1), (VZ, 6, 0, 1), (VZ, 7, 0, 1))
    + boxes((CXY, 7, 0, 1), (CXZ, 7, 0, 1))
    + boxes((RX, 6, -1, 1), (RX, 7, -1, 1), (RY, 6, -2, 2), (RY, 7, -2, 2), (RZ, 6, -1, 1), (RZ, 7, -1, 1))
    + boxes((RX, 8, 0, 3), (RY, 8, 0, 2), (RY, 9, 0, 2), (RZ, 8, 0, 3), (RZ, 9, 0, 3)),
}
ONCE = {
    (1, 0): rows_x(QQ, 7) + rows_x(PUSH, 6, 7),
    (-1, 0): [xs(f, 0) for f in (PP, QQ, COH, FRI)] + rows_x(PUSH, 0, 1, 2),
    (0, 1): rows_y(QQ, 7) + rows_y(PUSH, 6, 7),
    (0, -1): [ys(f, 0) for f in (PP, QQ, COH, FRI)] + rows_y(PUSH, 0, 1, 2),
    (1, 1): boxes((QQ, 7, 7, 1), (PUSH, 7, 6, 2), (PUSH, 6, 7, 1)),
    (-1, -1): [some(f, 0, 0) for f in (PP, QQ, COH, FRI)]
    + boxes((PUSH, 0, 0, 3), (PUSH, 1, 0, 1), (PUSH, 2, 0, 1)),
    (-1, 1): boxes((QQ, 0, 7, 1), (PUSH, 0, 6, 2), (PUSH, 1, 7, 1), (PUSH, 2, 7, 1)),
    (1, -1): boxes((QQ, 7, 0, 1), (PUSH, 7, 0, 3), (PUSH, 6, 0, 1)),
}


def rows_of(items):
    return -(-sum(item[4] for item in items) // 8) * 8


def parts(table):
    fields = (VX, VY, VZ, RX, RY, RZ, PUSH)
    early = {d: [i for i in table[d] if i[0] in fields or d in CORNERS] for d in SIDES}
    return early, {d: [i for i in table[d] if i[0] not in fields] for d in FACES}


MESSAGES = [*parts({d: ONCE[d] + EACH_STEP[d] for d in SIDES}), *parts(EACH_STEP)]

PLACES = {}
used = 0
for kind, table in enumerate(MESSAGES):
    for side, sent in table.items():
        PLACES[kind, side] = (used, rows_of(sent), len(PLACES))
        used += rows_of(sent)
BUFFER_ROWS = used
N_MESSAGES = len(PLACES)


def kernel(
    n_gx,
    n_gy,
    velocity_in,
    stress_in,
    memory_in,
    material_in,
    anelastic_in,
    zone_in,
    absorb_in,
    cells_in,
    moment_in,
    cohesion_in,
    friction_in,
    velocity,
    stress,
    memory,
    ext,
    sent,
    received,
    material,
    anelastic,
    zone,
    absorb,
    cells,
    moment,
    cohesion_table,
    friction_table,
    source,
    weight,
    centre,
    send_sem,
    recv_sem,
    in_sem,
):
    gx, gy = lax.axis_index("gx"), lax.axis_index("gy")
    there = {}
    for dx, dy in SIDES:
        checks = []
        if dx:
            checks.append(gx > 0 if dx < 0 else gx < n_gx - 1)
        if dy:
            checks.append(gy > 0 if dy < 0 else gy < n_gy - 1)
        there[dx, dy] = checks[0] if len(checks) == 1 else jnp.logical_and(*checks)

    def device(d):
        return (gx + d[0], gy + d[1])

    barrier = pltpu.get_barrier_semaphore()
    for d in SIDES:

        @pl.when(there[d])
        def _():
            pl.semaphore_signal(barrier, 1, device_id=device(d), device_id_type=MESH)

    loads = []
    for k, (src, dst) in enumerate(
        (
            (stress_in, stress),
            (velocity_in, velocity),
            (memory_in, memory),
            (material_in, material),
            (anelastic_in, anelastic),
            (zone_in, zone),
            (absorb_in, absorb),
            (cells_in, cells),
            (moment_in, moment),
            (cohesion_in, cohesion_table),
            (friction_in, friction_table),
        )
    ):
        loads.append(pltpu.make_async_copy(src, dst, in_sem.at[k]))
        loads[-1].start()

    def spot(field, form, x, y, n):
        start = row(x, y)
        return ext.at[field, pl.ds(start, n) if form == "B" else pl.ds(start, n, stride=PITCH), :]

    def at(item):
        return spot(*item)

    def landed(item, d):
        field, form, x, y, n = item
        return (field, form, x - 8 * d[0], y - 8 * d[1], n)

    def copy_of(kind, d, sem_side):
        start, n, k = PLACES[kind, d]
        n = sum(item[4] for item in MESSAGES[kind][d])
        return pltpu.make_async_remote_copy(
            src_ref=sent.at[pl.ds(start, n)],
            dst_ref=received.at[pl.ds(start, n)],
            send_sem=send_sem.at[k],
            recv_sem=recv_sem.at[k],
            device_id=device(sem_side),
            device_id_type=MESH,
        )

    def pack(kind, sides):
        for d in sides:
            items = MESSAGES[kind][d]
            start = PLACES[kind, d][0]
            for item in items:
                sent[pl.ds(start, item[4]), :] = at(item)[...]
                start += item[4]

    def send(kind, sides):
        for d in sides:

            @pl.when(there[d])
            def _():
                copy_of(kind, d, d).start()

    def receive(kind):
        for d, items in MESSAGES[kind].items():
            back = (-d[0], -d[1])

            @pl.when(there[back])
            def _():
                copy_of(kind, d, back).wait_recv()
                start = PLACES[kind, d][0]
                for item in items:
                    value = received[pl.ds(start, item[4]), :]
                    start += item[4]
                    field, form, x, y, n = landed(item, d)
                    if field in (RX, RY, RZ) and 0 <= x < 8 and 0 <= y < 8:
                        mine = spot(field - RX + VX, form, x, y, n)
                        mine[...] = mine[...] + spot(PUSH, form, x, y, n)[...] * value
                    elif field in (RX, RY, RZ):
                        rates = spot(field, form, x, y, n)
                        rates[...] = rates[...] + value
                    else:
                        spot(field, form, x, y, n)[...] = value

    def outside(kind):
        for d, items in MESSAGES[kind].items():

            @pl.when(jnp.logical_not(there[-d[0], -d[1]]))
            def _():
                for item in items:
                    if item[0] not in (RX, RY, RZ):
                        value = OPEN if item[0] == COH else 0.0
                        spot(*landed(item, d))[...] = jnp.full((item[4], 128), value, jnp.float32)

    depth = lax.broadcasted_iota(jnp.int32, (8, 128), 1)

    def deeper(f, n):
        moved = pltpu.roll(f, (-n) % 128, 1)
        return jnp.where((depth < 128 - n) if n > 0 else (depth >= -n), moved, 0.0)

    def view(field, x, y, form):
        start = row(x, y)
        return ext[field, pl.ds(start, 8) if form == "B" else pl.ds(start, 8, stride=PITCH), :]

    def put(field, x, y, form, value):
        start = row(x, y)
        ext[field, pl.ds(start, 8) if form == "B" else pl.ds(start, 8, stride=PITCH), :] = value

    def along(field, x, y, form, axis, first):
        f = [
            view(field, x + (first + k if axis == 0 else 0), y + (first + k if axis == 1 else 0), form)
            for k in range(4)
        ]
        return NEAR * (f[2] - f[1]) + FAR * (f[3] - f[0])

    def forward(field, x, y, form, axis):
        return along(field, x, y, form, axis, -1)

    def backward(field, x, y, form, axis):
        return along(field, x, y, form, axis, -2)

    def forward_z(f):
        return NEAR * (deeper(f, 1) - f) + FAR * (deeper(f, 2) - deeper(f, -1))

    def backward_z(f):
        return NEAR * (f - deeper(f, -1)) + FAR * (deeper(f, 1) - deeper(f, -2))

    nothing = jnp.zeros((8, 128), jnp.float32)
    for field in (SXX, SXY, SXZ, SYY, SYZ):
        for x in (-2, -1, 8, 9):
            put(field, x, -4, "B", nothing)
            put(field, x, 4, "B", nothing)
        for y in (-2, -1, 8, 9):
            put(field, 0, y, "F", nothing)
    outside(0)
    outside(1)
    loads[0].wait()
    for x in range(8):
        for field, c in ((SXX, 0), (SXY, 3), (SXZ, 4), (SYY, 1), (SYZ, 5)):
            put(field, x, 0, "B", stress[c, x])

    for k, load in enumerate(loads):
        if k:
            load.wait()
    place = cells[0]
    column = lax.broadcasted_iota(jnp.int32, (64, 128), 0) == (place // 128)
    spread = jnp.concatenate(
        [jnp.where(column, H * moment[0, c], 0.0) for c in range(6)], axis=0
    )
    at_depth = (lax.broadcasted_iota(jnp.int32, (128, 128), 0) == (place % 128)).astype(jnp.float32)
    source[...] = lax.dot_general(
        spread,
        at_depth,
        (((1,), (1,)), ((), ())),
        precision=lax.Precision.HIGHEST,
        preferred_element_type=jnp.float32,
    )
    for x in range(8):
        damping = jnp.where(absorb[x] == 1, SPONGE, 1.0)
        weight[0, x] = damping
        put(PUSH, x, 0, "B", H * material[2, x] * damping)
        grown = 1.0 - 0.5 * anelastic[1, x]
        weight[2, x] = grown
        put(PP, x, 0, "B", H * grown * material[0, x])
        put(QQ, x, 0, "B", H * grown * material[1, x])
        cohesion = jnp.zeros((8, 128), jnp.float32)
        friction = jnp.zeros((8, 128), jnp.float32)
        for z in range(ZONES):
            inside = zone[x] == z
            cohesion = jnp.where(inside, cohesion_table[z], cohesion)
            friction = jnp.where(inside, friction_table[z], friction)
        put(COH, x, 0, "B", cohesion)
        put(FRI, x, 0, "B", friction)

    ALL = (CXX, CYY, CZZ, CXY, CXZ, CYZ)
    F_STARTS = (-1, 1)

    for step in range(STEPS):
        kind = 2 * step
        for x in range(8):
            keep = 0.5 + 0.5 * anelastic[0, x]
            for c, field in enumerate(ALL):
                base = stress[c, x] + source[pl.ds(c * 64 + x * 8, 8), :] - keep * memory[c, x]
                put(field, x, 0, "B", base)
        for field in (RX, RY, RZ):
            for x in (-2, -1, 8, 9, 10):
                put(field, x, -4, "B", nothing)
                put(field, x, 4, "B", nothing)
        for field, source_field, axis, reach in (
            (RX, SXX, 0, -1),
            (RY, SXY, 0, -2),
            (RZ, SXZ, 0, -2),
            (RY, SYY, 1, -1),
            (RX, SXY, 1, -2),
            (RZ, SYZ, 1, -2),
        ):
            factors = (-FAR, -NEAR, NEAR, FAR)
            for i in (-2, -1, 8, 9, 10):
                total = None
                for k in range(4):
                    j = i + reach + k
                    if 0 <= j < 8:
                        term = factors[k] * (
                            view(source_field, j, 0, "B") if axis == 0 else view(source_field, 0, j, "F")
                        )
                        total = term if total is None else total + term
                if axis == 0:
                    if total is not None:
                        put(field, i, 0, "B", total)
                else:
                    put(field, 0, i, "F", nothing if total is None else total)
        for x in range(8):
            rate_x = (
                forward(SXX, x, 0, "B", 0) + backward(SXY, x, 0, "B", 1) + backward_z(stress[4, x])
            )
            rate_y = (
                backward(SXY, x, 0, "B", 0) + forward(SYY, x, 0, "B", 1) + backward_z(stress[5, x])
            )
            rate_z = (
                backward(SXZ, x, 0, "B", 0) + backward(SYZ, x, 0, "B", 1) + forward_z(stress[2, x])
            )
            damping, push = weight[0, x], view(PUSH, x, 0, "B")
            for c, (field, rate) in enumerate(((VX, rate_x), (VY, rate_y), (VZ, rate_z))):
                before = view(field, x, 0, "B") if step else velocity[c, x]
                put(field, x, 0, "B", before * damping + push * rate)
        pack(kind, CORNERS)
        if step == 0:
            pack(kind, FACES)
            pack(kind + 1, FACES)
            pl.semaphore_wait(barrier, sum(there[d].astype(jnp.int32) for d in SIDES))
        send(kind, CORNERS)
        for part in (kind, kind + 1):
            for d in FACES:
                if step:
                    pack(part, [d])
                send(part, [d])
        last = step == STEPS - 1
        receive(kind)
        for field, rates in ((VX, RX), (VY, RY), (VZ, RZ)):
            beside = [(x, y, "B") for x in (-2, -1, 8, 9, 10) for y in (-4, 4)]
            for x, y, form in beside + [(0, y, "F") for y in (-2, -1, 8, 9, 10)]:
                new = view(field, x, y, form) + view(PUSH, x, y, form) * view(rates, x, y, form)
                put(field, x, y, form, new)
        if last:
            for x in range(8):
                for c, field in enumerate((VX, VY, VZ)):
                    velocity[c, x] = view(field, x, 0, "B")

        def shear_xy(x, y, form):
            return forward(VX, x, y, form, 1) + forward(VY, x, y, form, 0)

        def shear_xz(x, y, form):
            return forward_z(view(VX, x, y, form)) + forward(VZ, x, y, form, 0)

        def shear_yz(x, y, form):
            return forward_z(view(VY, x, y, form)) + forward(VZ, x, y, form, 1)

        def normal(x, y, form):
            return (
                backward(VX, x, y, form, 0),
                backward(VY, x, y, form, 1),
                backward_z(view(VZ, x, y, form)),
            )

        def put_shear(field, x, y, form, value):
            put(field, x, y, form, value if field == TXY else value + deeper(value, -1))

        def keep_centre(k, x, y, form, trial):
            mean = (trial[0] + trial[1] + trial[2]) * (1.0 / 3.0)
            dev = [t - mean for t in trial]
            cohesion = view(COH, x, y, form)
            limit = jnp.maximum(cohesion - view(FRI, x, y, form) * mean, 0.25 * cohesion)
            centre[k, 0] = 0.5 * (dev[0] * dev[0] + dev[1] * dev[1] + dev[2] * dev[2])
            centre[k, 1] = limit
            if k < 8:
                centre[k, 2] = mean
                for c in range(3):
                    centre[k, 3 + c] = dev[c]

        for x in range(8):
            parts = normal(x, 0, "B")
            volume = parts[0] + parts[1] + parts[2]
            lame, modulus = H * material[0, x], H * material[1, x]
            spread_out = lame * volume
            rates = [spread_out + 2.0 * modulus * e for e in parts] + [
                modulus * e
                for e in (shear_xy(x, 0, "B"), shear_xz(x, 0, "B"), shear_yz(x, 0, "B"))
            ]
            grown, decay, share = weight[2, x], anelastic[0, x], anelastic[1, x]
            trial = []
            for c, field in enumerate(ALL):
                trial.append(view(field, x, 0, "B") + grown * rates[c])
                memory[c, x] = decay * memory[c, x] + share * rates[c]
            for c, field in ((3, TXY), (4, UXZ), (5, UYZ)):
                put_shear(field, x, 0, "B", trial[c])
                centre[x, 3 + c] = trial[c]
            keep_centre(x, x, 0, "B", trial[:3])
        receive(kind + 1)
        beyond = [(8, 8, 0, "B")] + [(9 + k, x, 8, "F") for k, x in enumerate(F_STARTS)]
        for k, x, y, form in beyond:
            parts = normal(x, y, form)
            volume = parts[0] + parts[1] + parts[2]
            lame, modulus = view(PP, x, y, form), view(QQ, x, y, form)
            trial = [
                view(field, x, y, form) + lame * volume + 2.0 * modulus * e
                for field, e in zip(ALL, parts)
            ]
            keep_centre(k, x, y, form, trial)
            for field, base, e in (
                (TXY, CXY, shear_xy(x, y, form)),
                (UXZ, CXZ, shear_xz(x, y, form)),
                (UYZ, CYZ, shear_yz(x, y, form)),
            ):
                put_shear(field, x, y, form, view(base, x, y, form) + modulus * e)
        modulus = view(QQ, -1, 0, "B")
        put_shear(TXY, -1, 0, "B", view(CXY, -1, 0, "B") + modulus * shear_xy(-1, 0, "B"))
        put_shear(UXZ, -1, 0, "B", view(CXZ, -1, 0, "B") + modulus * shear_xz(-1, 0, "B"))
        for x in F_STARTS:
            modulus = view(QQ, x, -1, "F")
            put_shear(TXY, x, -1, "F", view(CXY, x, -1, "F") + modulus * shear_xy(x, -1, "F"))
            put_shear(UYZ, x, -1, "F", view(CYZ, x, -1, "F") + modulus * shear_yz(x, -1, "F"))

        for k, x, y, form in [(x, x, 0, "B") for x in range(8)] + beyond:
            mean_xy = 0.25 * (
                (view(TXY, x - 1, y - 1, form) + view(TXY, x - 1, y, form))
                + (view(TXY, x, y - 1, form) + view(TXY, x, y, form))
            )
            mean_xz = 0.25 * (view(UXZ, x - 1, y, form) + view(UXZ, x, y, form))
            mean_yz = 0.25 * (view(UYZ, x, y - 1, form) + view(UYZ, x, y, form))
            tau = jnp.sqrt(
                centre[k, 0] + mean_xy * mean_xy + mean_xz * mean_xz + mean_yz * mean_yz
            )
            ratio = jnp.minimum(1.0, centre[k, 1] / jnp.maximum(tau, 0.5))
            deficit = 1.0 - ratio
            put(DEF, x, y, form, deficit)
            put(DEZ, x, y, form, deficit + deeper(deficit, 1))
            if k < 8:
                centre[k, 1] = ratio

        for x in range(8):
            ratio, mean = centre[x, 1], centre[x, 2]
            new = [mean + ratio * centre[x, 3 + c] for c in range(3)]
            lack = [view(DEF, x + i, j, "B") for i in (0, 1) for j in (0, 1)]
            new.append((1.0 - 0.25 * ((lack[0] + lack[1]) + (lack[2] + lack[3]))) * centre[x, 6])
            here = view(DEZ, x, 0, "B")
            new.append((1.0 - 0.25 * (here + view(DEZ, x + 1, 0, "B"))) * centre[x, 7])
            new.append((1.0 - 0.25 * (here + view(DEZ, x, 1, "B"))) * centre[x, 8])
            for c in range(6):
                stress[c, x] = new[c]
            if not last:
                for field, c in ((SXX, 0), (SXY, 3), (SXZ, 4), (SYY, 1), (SYZ, 5)):
                    put(field, x, 0, "B", new[c])

    for kind, table in enumerate(MESSAGES):
        for d in table:

            @pl.when(there[d])
            def _():
                copy_of(kind, d, d).wait_send()


def hand_over(*refs):
    n = (len(refs) - 1) // 2
    copies = [pltpu.make_async_copy(refs[k], refs[n + k], refs[-1].at[k]) for k in range(n)]
    for copy in copies:
        copy.start()
    for copy in copies:
        copy.wait()


def shards(
    n_gx,
    n_gy,
    velocity,
    stress,
    memory,
    material,
    anelastic,
    zone_ids,
    absorb_mask,
    source_cells,
    source_moment,
    cohesion_table,
    friction_table,
):
    far = pl.BlockSpec(memory_space=pl.ANY)
    near = pl.BlockSpec(memory_space=pltpu.VMEM)
    f32, i32 = jnp.float32, jnp.int32
    block = (8, 8, 128)
    operands = (
        velocity,
        stress,
        memory,
        material,
        anelastic,
        zone_ids,
        absorb_mask,
        source_cells,
        jnp.swapaxes(source_moment, 1, 2),
        cohesion_table,
        friction_table,
    )
    results = pl.pallas_call(
        functools.partial(kernel, n_gx, n_gy),
        out_shape=[pltpu.VMEM((n, *block), f32) for n in (3, 6, 6)],
        in_specs=[far] * 11,
        out_specs=[near] * 3,
        scratch_shapes=[
            pltpu.VMEM((FIELDS, SLABS * PITCH, 128), f32),
            pltpu.VMEM((BUFFER_ROWS, 128), f32),
            pltpu.VMEM((BUFFER_ROWS, 128), f32),
            pltpu.VMEM((3, *block), f32),
            pltpu.VMEM((2, *block), f32),
            pltpu.VMEM(block, i32),
            pltpu.VMEM(block, i32),
            pltpu.VMEM((1, 1, 128), i32),
            pltpu.VMEM((1, 6, 1, 128), f32),
            pltpu.SMEM((ZONES,), f32),
            pltpu.SMEM((ZONES,), f32),
            pltpu.VMEM((6 * 64, 128), f32),
            pltpu.VMEM((3, *block), f32),
            pltpu.VMEM((11, 9, 8, 128), f32),
            pltpu.SemaphoreType.DMA((N_MESSAGES,)),
            pltpu.SemaphoreType.DMA((N_MESSAGES,)),
            pltpu.SemaphoreType.DMA((11,)),
        ],
        compiler_params=pltpu.CompilerParams(
            collective_id=0, has_side_effects=True, vmem_limit_bytes=32 * 2**20
        ),
        name="waves",
    )(*[pltpu.with_memory_space_constraint(x, pltpu.HBM) for x in operands])
    return tuple(
        pl.pallas_call(
            hand_over,
            out_shape=[jax.ShapeDtypeStruct(r.shape, r.dtype) for r in results],
            in_specs=[near] * 3,
            out_specs=[far] * 3,
            scratch_shapes=[pltpu.SemaphoreType.DMA((3,))],
            name="results",
        )(*[pltpu.with_memory_space_constraint(r, pltpu.VMEM) for r in results])
    )


def solution(mesh):
    in_specs = (
        P(None, "gx", "gy", None),
        P(None, "gx", "gy", None),
        P(None, "gx", "gy", None),
        P(None, "gx", "gy", None),
        P(None, "gx", "gy", None),
        P("gx", "gy", None),
        P("gx", "gy", None),
        P("gx", "gy", None),
        P("gx", "gy", None, None),
        P(),
        P(),
    )
    out_specs = (P(None, "gx", "gy", None), P(None, "gx", "gy", None), P(None, "gx", "gy", None))
    body = functools.partial(shards, mesh.shape["gx"], mesh.shape["gy"])
    return jax.shard_map(body, mesh=mesh, in_specs=in_specs, out_specs=out_specs, check_vma=False)
```
